256 devices in a mesh: dp: 128 (over x, y, z), sub: 2 (over core).
Axes of the slice: x: 4, y: 4, z: 8, core: 2. Of those that a mesh axis runs over, the one named last changes fastest.
Arguments:
- frames: bfloat16 [262144, 440], P(('dp', 'sub')), may hold values from -6 to 6
- freqs: bfloat16 [440, 1024], P(None, ('dp', 'sub')), may hold values from -0.38138504 to 0.38138504
- phase: float32 [1024], replicated, may hold values from -3.140625 to 3.140625
- labels: int32 [262144], P(('dp', 'sub')), may hold values from 0 to 146
- predictions: float32 [262144, 147], P(('dp', 'sub')), may hold values from -4 to 4
- coeffs_old: float32 [1024, 147], P(('dp', 'sub')), may hold values from -0.4 to 0.4
Outputs:
- new_predictions: float32 [262144, 147], P(('dp', 'sub'))
- coeffs_new: float32 [1024, 147], replicated
The draws below stay inside these ranges and needn't reach their ends.
All inputs are finite; a program needn't handle non-finite values.
Results may differ from the reference program's by a relative error of at most 0.0015.
The reference program's roundings to bfloat16 on the way (of `features`, `residual` and `change`) count: a program that leaves them out, or rounds other values in their place, can miss the bound.
Values may be sent and summed in bfloat16 or wider, within the bound.
No kernel may reach another device: no remote copies, remote signals or barrier semaphores. Data moves between devices by JAX's collectives and lax.ppermute only.
A program may use at most 64 MiB of HBM per device.

```python
import jax
import jax.numpy as jnp
from jax import lax

D_IN = 440
CLASSES = 147
BLK = 1024
R_DEV = 1024
NROWS = 262144


def draw_freqs(key, part):
    key = jax.random.fold_in(key, 7)
    scale_key, value_key = jax.random.split(key)
    log_scales = jax.random.uniform(scale_key, (BLK,), jnp.float32, jnp.log(0.2), jnp.log(2.0))
    values = jax.random.truncated_normal(value_key, -4.0, 4.0, (D_IN, BLK), jnp.float32)
    return (values * jnp.exp(log_scales)[None, :] / jnp.sqrt(jnp.float32(D_IN))).astype(jnp.bfloat16)


def place_ends(result, stream_key, least, largest):
    index_at = [jax.random.randint(jax.random.fold_in(stream_key, axis), (), 0, length) for axis, length in enumerate(result.shape)]
    main_axis = result.shape.index(max(result.shape))
    neighbour = index_at[:main_axis] + [(index_at[main_axis] + 1) % result.shape[main_axis]] + index_at[main_axis + 1:]
    return result.at[tuple(index_at)].set(least).at[tuple(neighbour)].set(largest)


def shard_levels(key, shape, cuts, least, high):
    factor_of = 1.0
    for axis_at, shards_of in cuts:
        draws = jax.random.uniform(jax.random.fold_in(jax.random.fold_in(key, 6), axis_at), (shards_of,), jnp.float32, least / len(cuts), high / len(cuts))
        factor_of = factor_of * jnp.repeat(jnp.exp(draws), shape[axis_at] // shards_of).reshape((-1,) + (1,) * (len(shape) - 1 - axis_at))
    return factor_of


def centred(own_key, shape, deviation, most, shards=(), kind=jnp.bfloat16):
    array = jax.random.normal(own_key, shape, jnp.float32) * deviation
    if len(shards) > 0:
        array = shard_levels(own_key, shape, shards, -0.22, 0.18) * array
    return jnp.clip(array, min=-most, max=most).astype(kind)


def setup_inputs(seed: int = 0) -> dict:
    streams_of = jax.random.split(jax.random.key(seed), 7)
    return {
        "frames": centred(streams_of[0], (NROWS, D_IN), 1.0, 6.0, ((0, 256),)),
        "freqs": draw_freqs(jax.random.fold_in(streams_of[6], 71), 0),
        "phase": jnp.clip(jax.random.uniform(streams_of[2], (BLK,), jnp.float32, -3.140625, 3.140625), -3.140625, 3.140625),
        "labels": place_ends(jax.random.randint(streams_of[3], (NROWS,), 0, CLASSES), jax.random.fold_in(streams_of[3], 1), 0, CLASSES - 1).astype(jnp.int32),
        "predictions": centred(streams_of[4], (NROWS, CLASSES), 0.5, 4.0, ((0, 256),), jnp.float32),
        "coeffs_old": centred(streams_of[5], (BLK, CLASSES), 0.05, 0.4, ((0, 256),), jnp.float32),
    }


root_two = 1.4142135623730951
ridge = 1.0

def features_of(block_frames, freqs, phase):
    angles = jnp.dot(block_frames.astype(jnp.float32), freqs.astype(jnp.float32), preferred_element_type=jnp.float32) + phase[None, :]
    return (root_two * jnp.cos(angles)).astype(jnp.bfloat16)

def residual_of(block_labels, block_preds):
    onehot = (block_labels[:, None] == jnp.arange(CLASSES, dtype=jnp.int32)[None, :]).astype(jnp.float32)
    return (onehot - block_preds).astype(jnp.bfloat16)

def reference(frames, freqs, phase, labels, predictions, coeffs_old):
    frame_blocks = frames.reshape(-1, R_DEV, D_IN)
    label_blocks = labels.reshape(-1, R_DEV)
    pred_blocks = predictions.reshape(-1, R_DEV, CLASSES)

    def accumulate(carry, items):
        gram, cross = carry
        block_frames, block_labels, block_preds = items
        features = features_of(block_frames, freqs, phase)
        residual = residual_of(block_labels, block_preds)
        gram = gram + jnp.dot(features.T.astype(jnp.float32), features.astype(jnp.float32), preferred_element_type=jnp.float32)
        cross = cross + jnp.dot(features.T.astype(jnp.float32), residual.astype(jnp.float32), preferred_element_type=jnp.float32)
        return ((gram, cross), None)
    start_carry = (jnp.zeros((BLK, BLK), jnp.float32), jnp.zeros((BLK, CLASSES), jnp.float32))
    (gram, cross), _ = lax.scan(accumulate, start_carry, (frame_blocks, label_blocks, pred_blocks))
    system = gram / NROWS + ridge * jnp.eye(BLK, dtype=jnp.float32)
    right_side = (cross + jnp.dot(gram.astype(jnp.float32), coeffs_old.astype(jnp.float32), precision=lax.Precision.HIGHEST, preferred_element_type=jnp.float32)) / NROWS
    factor = jnp.linalg.cholesky(system)
    halfway = lax.linalg.triangular_solve(factor, right_side, left_side=True, lower=True)
    coeffs_new = lax.linalg.triangular_solve(factor, halfway, left_side=True, lower=True, transpose_a=True)
    change = (coeffs_new - coeffs_old).astype(jnp.bfloat16)

    def update(items):
        block_frames, block_preds = items
        features = features_of(block_frames, freqs, phase)
        return block_preds + jnp.dot(features.astype(jnp.float32), change.astype(jnp.float32), preferred_element_type=jnp.float32)
    new_blocks = lax.map(update, (frame_blocks, pred_blocks))
    return (new_blocks.reshape(NROWS, CLASSES), coeffs_new)
```

```python
import functools

import jax
import jax.numpy as jnp
import numpy as np
from jax import lax
from jax.experimental import pallas as pl
from jax.experimental.pallas import tpu as pltpu
from jax.sharding import Mesh, PartitionSpec as P

f32 = jnp.float32
bf16 = jnp.bfloat16
root_two = 1.4142135623730951
ridge = 1.0
tile = 128
step = 256
NN = (((1,), (0,)), ((), ()))
NT = (((1,), (1,)), ((), ()))


def cosine_coefficients(degree):
    nodes = 0.125 * np.cos(np.pi * (np.arange(400) + 0.5) / 400) + 0.125
    wanted = root_two * np.cos(2 * np.pi * np.sqrt(nodes))
    fitted = np.polynomial.chebyshev.Chebyshev.fit(nodes, wanted, degree, domain=[0, 0.25])
    return [float(c) for c in fitted.convert(kind=np.polynomial.Polynomial).coef]


cosine = cosine_coefficients(6)


def features_of(angles):
    turns = angles * (0.5 / np.pi)
    part = turns - jnp.round(turns)
    square = part * part
    value = cosine[-1] * square + cosine[-2]
    for coefficient in cosine[-3::-1]:
        value = value * square + coefficient
    return value.astype(bf16)


def dot(a, b, dims=NN):
    return lax.dot_general(a, b, dims, preferred_element_type=f32)


def split(x):
    high = x.astype(bf16)
    return high, (x - high.astype(f32)).astype(bf16)


def product(a, b):
    return dot(a[0], b[0]) + (dot(a[0], b[1]) + dot(a[1], b[0]))


def pairs(blocks):
    return [(a, b) for a in range(blocks) for b in range(a + 1)]


def layout(width, classes):
    blocks = width // tile
    lower = len(pairs(blocks)) * tile
    each = (-(-(lower + blocks * classes) // 2048) * 2048 - lower) // blocks
    return blocks, lower, each, lower + blocks * each


def moment_kernel(frames, freqs, phase, labels, predictions, turned, packed, padded):
    width, (rows, classes) = freqs.shape[0], predictions.shape
    blocks, lower, each, _ = layout(width, classes)
    padded[...] = jnp.zeros_like(padded)
    padded[:, :classes] = predictions[...]
    onehot = labels[...] == lax.broadcasted_iota(jnp.int32, (padded.shape[1], rows), 0)
    residual = (onehot.astype(f32) - padded[...].T)[:each].astype(bf16)
    row = 0
    for i in range(width // step):
        mine = slice(i * step, (i + 1) * step)
        angles = dot(freqs[mine, : frames.shape[1]], frames[...], NT) + phase[mine, :]
        block = features_of(angles)
        turned[mine, :] = block
        gram = dot(block, turned[: (i + 1) * step, :], NT)
        cross = dot(residual, block, NT)
        for j in range(step // tile):
            a = i * (step // tile) + j
            for b in range(a + 1):
                packed[row : row + tile, :] = gram[j * tile : (j + 1) * tile, b * tile : (b + 1) * tile]
                row += tile
            packed[lower + a * each : lower + (a + 1) * each, :] = cross[:, j * tile : (j + 1) * tile]


def moments(frames, freqs, phase, labels, predictions):
    width, (rows, classes) = freqs.shape[0], predictions.shape
    _, _, _, total = layout(width, classes)
    here = pl.BlockSpec(memory_space=pltpu.VMEM)
    return pl.pallas_call(
        moment_kernel,
        out_shape=(
            jax.ShapeDtypeStruct((width, rows), bf16),
            jax.ShapeDtypeStruct((total, tile), f32),
        ),
        in_specs=[here] * 5,
        out_specs=(here, here),
        scratch_shapes=[pltpu.VMEM((rows, 2 * tile), f32)],
        compiler_params=pltpu.CompilerParams(vmem_limit_bytes=48 * 1024 * 1024),
        name="moments",
    )(frames, freqs, phase, labels, predictions)


def inverse(a, eye):
    bound = 2.0 * a.shape[0]
    scale = 2.0 / (2.0 * ridge + bound)
    spread = bound / (2.0 * ridge + bound)
    rest = eye - scale * a
    for k in range(7):
        gain = 2.0 / (2.0 - spread * spread)
        parts = split(rest)
        x = (gain * scale) * (eye + rest) if k == 0 else gain * (x + product(split(x), parts))
        spread = spread * spread / (2.0 - spread * spread)
        if k < 6:
            rest = gain * product(parts, parts) - spread * eye
    missing = eye - product(split(a), split(x))
    return x + product(split(x), split(missing))


def solve_kernel(
    total_rows, packed, old, turned, predictions, coeffs, updated,
    system, work, inv_h, inv_l, low_h, low_l, up_h, up_l, right, found,
):
    width = system.shape[0]
    classes = coeffs.shape[1]
    blocks, lower, each, _ = layout(width, classes)
    count = width // step
    scale = 1.0 / total_rows
    padded = right.shape[0]
    eye = (
        lax.broadcasted_iota(jnp.int32, (step, step), 0)
        == lax.broadcasted_iota(jnp.int32, (step, step), 1)
    ).astype(f32)
    for t, (a, b) in enumerate(pairs(blocks)):
        part = packed[t * tile : (t + 1) * tile, :] * scale
        if a == b:
            part = part + ridge * eye[:tile, :tile]
        system[a * tile : (a + 1) * tile, b * tile : (b + 1) * tile] = part
        if a != b:
            system[b * tile : (b + 1) * tile, a * tile : (a + 1) * tile] = part.T
    for m in range(blocks):
        lanes = slice(m * tile, (m + 1) * tile)
        start = lower + m * each
        right[:, lanes] = packed[start : start + padded, :] * scale - old[:, lanes]

    def at(k):
        return slice(k * step, (k + 1) * step)

    for k in range(count):
        source = system if k == 0 else work
        x = split(inverse(source[at(k), at(k)], eye))
        inv_h[at(k), :], inv_l[at(k), :] = x
        if k == count - 1:
            break
        after = slice((k + 1) * step, width)
        column = split(product(split(source[after, at(k)]), x))
        low_h[after, at(k)], low_l[after, at(k)] = column
        row = split(source[at(k), after])
        up_h[at(k), after], up_l[at(k), after] = row
        work[after, after] = source[after, after] - product(column, row)

    def apply(parts):
        parts = list(parts)
        for k in range(count):
            now = parts[k] = product(split(parts[k]), (inv_h[at(k), :], inv_l[at(k), :]))
            if k < count - 1:
                after = slice((k + 1) * step, width)
                less = product(split(now), (up_h[at(k), after], up_l[at(k), after]))
                for i in range(k + 1, count):
                    parts[i] = parts[i] - less[:, (i - k - 1) * step : (i - k) * step]
        for k in reversed(range(1, count)):
            before = slice(0, k * step)
            less = product(split(parts[k]), (low_h[at(k), before], low_l[at(k), before]))
            for i in range(k):
                parts[i] = parts[i] - less[:, i * step : (i + 1) * step]
        return parts

    for k, part in enumerate(apply([right[:, at(k)] for k in range(count)])):
        found[:, at(k)] = part
    for _ in range(2):
        short = right[...] - lax.dot_general(
            found[...], system[...], NN, precision=lax.Precision.HIGHEST, preferred_element_type=f32
        )
        for k, part in enumerate(apply([short[:, at(k)] for k in range(count)])):
            found[:, at(k)] += part
    change = found[...]
    empty = jnp.zeros((2 * tile - padded, width), f32)
    coeffs[...] = jnp.concatenate([old[...] + change, empty], axis=0).T[:, :classes]
    added = dot(change.astype(bf16), turned[...])
    empty = jnp.zeros((2 * tile - padded, turned.shape[1]), f32)
    updated[...] = predictions[...] + jnp.concatenate([added, empty], axis=0).T[:, :classes]


def solve(packed, old, turned, predictions, total_rows):
    width, (rows, classes) = turned.shape[0], predictions.shape
    here = pl.BlockSpec(memory_space=pltpu.VMEM)
    padded = old.shape[0]
    return pl.pallas_call(
        functools.partial(solve_kernel, float(total_rows)),
        out_shape=(
            jax.ShapeDtypeStruct((width, classes), f32),
            jax.ShapeDtypeStruct((rows, classes), f32),
        ),
        in_specs=[here] * 4,
        out_specs=(here, here),
        scratch_shapes=[
            pltpu.VMEM((width, width), f32),
            pltpu.VMEM((width, width), f32),
            pltpu.VMEM((width, step), bf16),
            pltpu.VMEM((width, step), bf16),
            pltpu.VMEM((width, width), bf16),
            pltpu.VMEM((width, width), bf16),
            pltpu.VMEM((width, width), bf16),
            pltpu.VMEM((width, width), bf16),
            pltpu.VMEM((padded, width), f32),
            pltpu.VMEM((padded, width), f32),
        ],
        compiler_params=pltpu.CompilerParams(vmem_limit_bytes=56 * 1024 * 1024),
        name="solve",
    )(packed, old, turned, predictions)


def exchange(x, axis):
    return lax.all_to_all(x, axis, 0, 0, tiled=True)


def spread_out(x, axes):
    for axis in reversed(axes):
        x = exchange(jnp.broadcast_to(x[None], (lax.axis_size(axis), *x.shape)), axis)
    return x


def add_up(x):
    rows, lanes = x.shape
    for axis in ("core", "x", "y", "z"):
        n = lax.axis_size(axis)
        x = exchange(x.reshape(n, -1, lanes), axis).sum(0)
    return spread_out(x, ("core", "x", "y", "z")).reshape(rows, lanes)


def local(frames, freqs, phase, labels, predictions, coeffs_old):
    rows, classes = predictions.shape
    depth, own = freqs.shape
    width = phase.shape[0]
    devices = width // own
    first = lax.reduce_precision(coeffs_old, 8, 7)
    second = lax.reduce_precision(coeffs_old - first, 8, 7)
    third = coeffs_old - first - second
    first, second, third = (part.astype(bf16) for part in (first, second, third))
    filled = depth + 3 * classes
    sent = jnp.concatenate(
        [freqs.T, first, second, third, jnp.zeros((own, -filled % tile), bf16)], axis=1
    )
    everything = spread_out(sent, ("core", "x", "y", "z"))
    everything = jnp.moveaxis(everything, 0, 3).reshape(width, sent.shape[1])
    parts = [everything[:, depth + i * classes : depth + (i + 1) * classes].astype(f32) for i in range(3)]
    old = (parts[0] + parts[1]) + parts[2]
    old = jnp.pad(old.T, ((0, -classes % 32), (0, 0)))
    turned, packed = moments(
        frames, everything, phase[:, None], labels[None, :], predictions
    )
    packed = add_up(packed)
    coeffs_new, new_predictions = solve(packed, old, turned, predictions, rows * devices)
    return new_predictions, coeffs_new


def solution(mesh):
    chips = mesh.devices.reshape(4, 4, 8, 2)
    inner = Mesh(chips, ("x", "y", "z", "core"))
    every = ("x", "y", "z", "core")
    placed = (P(every, None), P(None, every), P(), P(every), P(every, None), P(every, None))
    return jax.shard_map(
        local, mesh=inner, in_specs=placed, out_specs=(P(every, None), P()), check_vma=False
    )
```

```python
import functools

import jax
import jax.numpy as jnp
import numpy as np
from jax import lax
from jax.experimental import pallas as pl
from jax.experimental.pallas import tpu as pltpu
from jax.sharding import Mesh, PartitionSpec as P

f32 = jnp.float32
bf16 = jnp.bfloat16
root_two = 1.4142135623730951
ridge = 1.0
tile = 128
step = 256
own_width = 4
NN = (((1,), (0,)), ((), ()))
NT = (((1,), (1,)), ((), ()))


def cosine_coefficients(degree):
    nodes = 0.125 * np.cos(np.pi * (np.arange(400) + 0.5) / 400) + 0.125
    wanted = root_two * np.cos(2 * np.pi * np.sqrt(nodes))
    fitted = np.polynomial.chebyshev.Chebyshev.fit(nodes, wanted, degree, domain=[0, 0.25])
    return [float(c) for c in fitted.convert(kind=np.polynomial.Polynomial).coef]


cosine = cosine_coefficients(6)


def features_of(angles):
    turns = angles * (0.5 / np.pi)
    part = turns - jnp.round(turns)
    square = part * part
    value = cosine[-1] * square + cosine[-2]
    for coefficient in cosine[-3::-1]:
        value = value * square + coefficient
    return value.astype(bf16)


def dot(a, b, dims=NN):
    return lax.dot_general(a, b, dims, preferred_element_type=f32)


def split(x):
    high = x.astype(bf16)
    return high, (x - high.astype(f32)).astype(bf16)


def product(a, b):
    return dot(a[0], b[0]) + (dot(a[0], b[1]) + dot(a[1], b[0]))


def pairs(blocks):
    return [(a, b) for a in range(blocks) for b in range(a + 1)]


def layout(width, classes):
    blocks = width // tile
    lower = len(pairs(blocks)) * tile
    each = (-(-(lower + blocks * classes) // 2048) * 2048 - lower) // blocks
    return blocks, lower, each, lower + blocks * each


def moment_kernel(
    total_rows, place, mine, other, frames, phase, labels, predictions, own, turned, keep, send,
    packed, residual, sems,
):
    width, (classes, rows) = phase.shape[0], predictions.shape
    depth = frames.shape[0]
    blocks, lower, each, total = layout(width, classes)
    half = total // 2
    core, x = place[0], place[1]
    residual[...] = jnp.zeros_like(residual)
    onehot = labels[...] == lax.broadcasted_iota(jnp.int32, (classes, rows), 0)
    residual[:classes, :] = onehot.astype(f32) - predictions[...]
    wanted = residual[...].astype(bf16)
    row = 0
    for i in range(width // step):
        here = slice(i * step, (i + 1) * step)
        first = (i * step) % (width // 2)
        side = core == (i * step) // (width // 2)
        freqs = jnp.where(side, mine[first : first + step, :], other[first : first + step, :])
        angles = dot(freqs[:, :depth], frames[...]) + phase[here, :]
        block = features_of(angles)
        turned[here, :] = block
        gram = dot(block, turned[: (i + 1) * step, :], NT)
        cross = dot(wanted, block, NT)
        for j in range(step // tile):
            a = i * (step // tile) + j
            for b in range(a + 1):
                packed[row // half, row % half : row % half + tile, :] = gram[
                    j * tile : (j + 1) * tile, b * tile : (b + 1) * tile
                ]
                row += tile
            start = lower + a * each - half
            packed[1, start : start + each, :] = cross[:, j * tile : (j + 1) * tile]
    start = pl.multiple_of(lower - half + each * (core * (blocks // 2) + x), 8)
    packed[1, pl.ds(start, each), :] -= own[...] * total_rows
    copies = [
        pltpu.make_async_copy(packed.at[core], keep, sems.at[0]),
        pltpu.make_async_copy(packed.at[1 - core], send, sems.at[1]),
    ]
    for copy in copies:
        copy.start()
    for copy in copies:
        copy.wait()


def moments(place, mine, other, frames, phase, labels, predictions, own, total_rows):
    width, (classes, rows) = phase.shape[0], predictions.shape
    _, _, each, total = layout(width, classes)
    here = pl.BlockSpec(memory_space=pltpu.VMEM)
    half = jax.ShapeDtypeStruct((total // 2, tile), f32)
    return pl.pallas_call(
        functools.partial(moment_kernel, float(total_rows)),
        out_shape=(jax.ShapeDtypeStruct((width, rows), bf16), half, half),
        in_specs=[pl.BlockSpec(memory_space=pltpu.SMEM)] + [here] * 7,
        out_specs=(here, pl.BlockSpec(memory_space=pl.ANY), pl.BlockSpec(memory_space=pl.ANY)),
        scratch_shapes=[
            pltpu.VMEM((2, total // 2, tile), f32),
            pltpu.VMEM((each, rows), f32),
            pltpu.SemaphoreType.DMA((2,)),
        ],
        compiler_params=pltpu.CompilerParams(vmem_limit_bytes=40 * 1024 * 1024),
        name="moments",
    )(place, mine, other, frames, phase, labels, predictions, own)


def inverse(a, eye):
    bound = 2.0 * a.shape[0]
    scale = 2.0 / (2.0 * ridge + bound)
    spread = bound / (2.0 * ridge + bound)
    rest = eye - scale * a
    for k in range(7):
        gain = 2.0 / (2.0 - spread * spread)
        parts = split(rest)
        x = (gain * scale) * (eye + rest) if k == 0 else gain * (x + product(split(x), parts))
        spread = spread * spread / (2.0 - spread * spread)
        if k < 6:
            rest = gain * product(parts, parts) - spread * eye
    missing = eye - product(split(a), split(x))
    return x + product(split(x), split(missing))


def solve_kernel(
    total_rows, place, mine, other, old, turned, predictions, coeffs, updated,
    system, work, inv_h, inv_l, low_h, low_l, up_h, up_l, right, found,
):
    width = system.shape[0]
    classes = predictions.shape[0]
    blocks, lower, each, total = layout(width, classes)
    count = width // step
    scale = 1.0 / total_rows
    padded = right.shape[0]
    core = place[0]

    def sums(start, rows):
        part, start = divmod(start, total // 2)
        there = slice(start, start + rows)
        return jnp.where(core == part, mine[there, :], other[there, :])

    eye = (
        lax.broadcasted_iota(jnp.int32, (step, step), 0)
        == lax.broadcasted_iota(jnp.int32, (step, step), 1)
    ).astype(f32)
    for t, (a, b) in enumerate(pairs(blocks)):
        part = sums(t * tile, tile) * scale
        if a == b:
            part = part + ridge * eye[:tile, :tile]
        system[a * tile : (a + 1) * tile, b * tile : (b + 1) * tile] = part
        if a != b:
            system[b * tile : (b + 1) * tile, a * tile : (a + 1) * tile] = part.T
    for m in range(blocks):
        right[:, m * tile : (m + 1) * tile] = sums(lower + m * each, padded) * scale

    def at(k):
        return slice(k * step, (k + 1) * step)

    for k in range(count):
        source = system if k == 0 else work
        x = split(inverse(source[at(k), at(k)], eye))
        inv_h[at(k), :], inv_l[at(k), :] = x
        if k == count - 1:
            break
        after = slice((k + 1) * step, width)
        column = split(product(split(source[after, at(k)]), x))
        low_h[after, at(k)], low_l[after, at(k)] = column
        row = split(source[at(k), after])
        up_h[at(k), after], up_l[at(k), after] = row
        work[after, after] = source[after, after] - product(column, row)

    def apply(parts):
        parts = list(parts)
        for k in range(count):
            now = parts[k] = product(split(parts[k]), (inv_h[at(k), :], inv_l[at(k), :]))
            if k < count - 1:
                after = slice((k + 1) * step, width)
                less = product(split(now), (up_h[at(k), after], up_l[at(k), after]))
                for i in range(k + 1, count):
                    parts[i] = parts[i] - less[:, (i - k - 1) * step : (i - k) * step]
        for k in reversed(range(1, count)):
            before = slice(0, k * step)
            less = product(split(parts[k]), (low_h[at(k), before], low_l[at(k), before]))
            for i in range(k):
                parts[i] = parts[i] - less[:, i * step : (i + 1) * step]
        return parts

    for k, part in enumerate(apply([right[:, at(k)] for k in range(count)])):
        found[:, at(k)] = part
    for _ in range(2):
        short = right[...] - lax.dot_general(
            found[...], system[...], NN, precision=lax.Precision.HIGHEST, preferred_element_type=f32
        )
        for k, part in enumerate(apply([short[:, at(k)] for k in range(count)])):
            found[:, at(k)] += part
    change = found[...]
    added = dot(change.astype(bf16), turned[...])
    updated[...] = predictions[...] + added[:classes]
    at_row = lax.broadcasted_iota(jnp.int32, (2 * tile, 2 * tile), 0)
    at_lane = lax.broadcasted_iota(jnp.int32, (2 * tile, 2 * tile), 1)
    goal = (at_row % tile) // own_width * (2 * own_width) + at_row // tile * own_width + at_row % own_width
    order = (goal == at_lane).astype(bf16)
    early = old[pl.ds(0, width, stride=2), :]
    late = old[pl.ds(1, width, stride=2), :]
    for u in range(width // (2 * tile)):
        one, two = slice(u * tile, (u + 1) * tile), slice(width // 2 + u * tile, width // 2 + (u + 1) * tile)
        lanes = slice(2 * u * tile, 2 * (u + 1) * tile)
        part = jnp.concatenate([found[:, one], found[:, two]], axis=1)
        high, low = split(part)
        last = (part - high.astype(f32) - low.astype(f32)).astype(bf16)
        moved = (dot(high, order) + dot(low, order)) + dot(last, order)
        coeffs[:tile, lanes] = moved[:tile] + early[lanes].T
        coeffs[tile:, lanes] = moved[tile:classes] + late[lanes].T[: classes - tile]


def solve(place, mine, other, old, turned, predictions, total_rows):
    width, (classes, rows) = turned.shape[0], predictions.shape
    here = pl.BlockSpec(memory_space=pltpu.VMEM)
    padded = -(-classes // 16) * 16
    return pl.pallas_call(
        functools.partial(solve_kernel, float(total_rows)),
        out_shape=(
            jax.ShapeDtypeStruct((classes, width), f32),
            jax.ShapeDtypeStruct((classes, rows), f32),
        ),
        in_specs=[pl.BlockSpec(memory_space=pltpu.SMEM)] + [here] * 5,
        out_specs=(here, here),
        scratch_shapes=[
            pltpu.VMEM((width, width), f32),
            pltpu.VMEM((width, width), f32),
            pltpu.VMEM((width, step), bf16),
            pltpu.VMEM((width, step), bf16),
            pltpu.VMEM((width, width), bf16),
            pltpu.VMEM((width, width), bf16),
            pltpu.VMEM((width, width), bf16),
            pltpu.VMEM((width, width), bf16),
            pltpu.VMEM((padded, width), f32),
            pltpu.VMEM((padded, width), f32),
        ],
        compiler_params=pltpu.CompilerParams(vmem_limit_bytes=48 * 1024 * 1024),
        name="solve",
    )(place, mine, other, old, turned, predictions)


def exchange(x, axes):
    return lax.all_to_all(x, axes, 0, 0, tiled=True)


def gather(x, axes):
    return exchange(jnp.broadcast_to(x[None], (lax.axis_size(axes), *x.shape)), axes)


def swap(x):
    return lax.ppermute(x, "core", [(0, 1), (1, 0)])


def local(frames, freqs, phase, labels, predictions, coeffs_old):
    rows, classes = predictions.shape
    depth, own = freqs.shape
    width = phase.shape[0]
    cores = lax.axis_size("core")
    devices = width // own
    x, y, z = (lax.axis_index(axis) for axis in ("x", "y", "z"))
    place = jnp.stack([lax.axis_index("core"), x]).astype(jnp.int32)
    sent = jnp.pad(freqs.T, ((0, 0), (0, -depth % tile)))
    mine = gather(sent, "z").reshape(-1, sent.shape[1])
    mine = gather(mine, ("x", "y")).reshape(width // cores, sent.shape[1])
    other = swap(mine)
    old = jnp.pad(coeffs_old, ((0, 0), (0, -classes % tile))).reshape(-1, tile)
    old = lax.all_gather(old, ("x", "y", "z", "core"), axis=0, tiled=True)
    phase = phase.reshape(devices // cores, cores, own).swapaxes(0, 1).reshape(width, 1)
    _, _, each, total = layout(width, classes)
    owned = jnp.zeros((each, tile), f32)
    owned = lax.dynamic_update_slice(
        owned, coeffs_old.T, (0, (y * lax.axis_size("z") + z) * own)
    )
    turned, keep, send = moments(
        place, mine, other, frames.T, phase, labels[None, :], predictions.T, owned, rows * devices
    )
    sums = (keep + swap(send)).reshape(lax.axis_size(("x", "y")), -1, tile)
    sums = exchange(sums, ("x", "y")).sum(0)
    sums = exchange(sums.reshape(lax.axis_size("z"), -1, tile), "z").sum(0)
    sums = gather(sums, "z").reshape(-1, tile)
    mine = gather(sums, ("x", "y")).reshape(-1, tile)
    other = swap(mine)
    coeffs_new, new_predictions = solve(
        place, mine, other, old, turned, predictions.T, rows * devices
    )
    return new_predictions.T, coeffs_new.T


def solution(mesh):
    chips = mesh.devices.reshape(4, 4, 8, 2)
    inner = Mesh(chips, ("x", "y", "z", "core"))
    every = ("x", "y", "z", "core")
    placed = (P(every, None), P(None, every), P(), P(every), P(every, None), P(every, None))
    return jax.shard_map(
        local, mesh=inner, in_specs=placed, out_specs=(P(every, None), P()), check_vma=False
    )
```

```python
import functools

import jax
import jax.numpy as jnp
import numpy as np
from jax import lax
from jax.experimental import pallas as pl
from jax.experimental.pallas import tpu as pltpu
from jax.sharding import Mesh, PartitionSpec as P

f32 = jnp.float32
bf16 = jnp.bfloat16
root_two = 1.4142135623730951
ridge = 1.0
tile = 128
step = 256
own_width = 4
depth_of = 440
NN = (((1,), (0,)), ((), ()))
NT = (((1,), (1,)), ((), ()))


def cosine_coefficients(degree):
    nodes = 0.125 * np.cos(np.pi * (np.arange(400) + 0.5) / 400) + 0.125
    wanted = root_two * np.cos(2 * np.pi * np.sqrt(nodes))
    fitted = np.polynomial.chebyshev.Chebyshev.fit(nodes, wanted, degree, domain=[0, 0.25])
    return [float(c) for c in fitted.convert(kind=np.polynomial.Polynomial).coef]


cosine = cosine_coefficients(6)


def features_of(angles):
    turns = angles * (0.5 / np.pi)
    part = turns - jnp.round(turns)
    square = part * part
    value = cosine[-1] * square + cosine[-2]
    for coefficient in cosine[-3::-1]:
        value = value * square + coefficient
    return value.astype(bf16)


def dot(a, b, dims=NN):
    return lax.dot_general(a, b, dims, preferred_element_type=f32)


def split(x):
    high = x.astype(bf16)
    return high, (x - high.astype(f32)).astype(bf16)


def product(a, b):
    return dot(a[0], b[0]) + (dot(a[0], b[1]) + dot(a[1], b[0]))


def pairs(blocks):
    return [(a, b) for a in range(blocks) for b in range(a + 1)]


def layout(width, classes):
    blocks = width // tile
    lower = len(pairs(blocks)) * tile
    each = (-(-(lower + blocks * classes) // 2048) * 2048 - lower) // blocks
    return blocks, lower, each, lower + blocks * each


def moment_kernel(
    place, mine, other, frames, phase, labels, predictions, turned, keep, send,
    packed, residual, sems,
):
    width, (classes, rows) = phase.shape[0], predictions.shape
    depth = frames.shape[0]
    blocks, lower, each, total = layout(width, classes)
    half = total // 2
    core = place[0]
    residual[...] = jnp.zeros_like(residual)
    onehot = labels[...] == lax.broadcasted_iota(jnp.int32, (classes, rows), 0)
    residual[:classes, :] = onehot.astype(f32) - predictions[...]
    wanted = residual[...].astype(bf16)
    row = 0
    for i in range(width // step):
        here = slice(i * step, (i + 1) * step)
        first = (i * step) % (width // 2)
        side = core == (i * step) // (width // 2)
        there = slice(first, first + step)
        freqs = jnp.where(side, mine[there, :depth], other[there, :depth])
        angles = dot(freqs, frames[...]) + phase[here, :]
        block = features_of(angles)
        turned[here, :] = block
        gram = dot(block, turned[: (i + 1) * step, :], NT)
        cross = dot(wanted, block, NT)
        for j in range(step // tile):
            a = i * (step // tile) + j
            for b in range(a + 1):
                packed[row // half, row % half : row % half + tile, :] = gram[
                    j * tile : (j + 1) * tile, b * tile : (b + 1) * tile
                ]
                row += tile
            start = lower + a * each - half
            packed[1, start : start + each, :] = cross[:, j * tile : (j + 1) * tile]
    copies = [
        pltpu.make_async_copy(packed.at[core], keep, sems.at[0]),
        pltpu.make_async_copy(packed.at[1 - core], send, sems.at[1]),
    ]
    for copy in copies:
        copy.start()
    for copy in copies:
        copy.wait()


def moments(place, mine, other, frames, phase, labels, predictions):
    width, (classes, rows) = phase.shape[0], predictions.shape
    _, _, each, total = layout(width, classes)
    here = pl.BlockSpec(memory_space=pltpu.VMEM)
    half = jax.ShapeDtypeStruct((total // 2, tile), f32)
    return pl.pallas_call(
        moment_kernel,
        out_shape=(jax.ShapeDtypeStruct((width, rows), bf16), half, half),
        in_specs=[pl.BlockSpec(memory_space=pltpu.SMEM)] + [here] * 6,
        out_specs=(here, pl.BlockSpec(memory_space=pl.ANY), pl.BlockSpec(memory_space=pl.ANY)),
        scratch_shapes=[
            pltpu.VMEM((2, total // 2, tile), f32),
            pltpu.VMEM((each, rows), f32),
            pltpu.SemaphoreType.DMA((2,)),
        ],
        compiler_params=pltpu.CompilerParams(vmem_limit_bytes=40 * 1024 * 1024),
        name="moments",
    )(place, mine, other, frames, phase, labels, predictions)


def inverse(a, eye):
    bound = 2.0 * a.shape[0]
    scale = 2.0 / (2.0 * ridge + bound)
    spread = bound / (2.0 * ridge + bound)
    rest = eye - scale * a
    x = scale * eye
    for k in range(7):
        gain = 2.0 / (2.0 - spread * spread)
        parts = split(rest)
        spread = spread * spread / (2.0 - spread * spread)
        if k == 0:
            x = gain * (x + scale * rest)
            rest = gain * product(parts, parts) - spread * eye
        else:
            x = gain * (x + product(split(x), parts))
            if k < 6:
                rest = gain * product(parts, parts) - spread * eye
    missing = eye - product(split(a), split(x))
    return x + product(split(x), split(missing))


def solve_kernel(
    total_rows, place, mine, other, mine_old, other_old, turned, predictions, coeffs, updated,
    system, work, inv_h, inv_l, low_h, low_l, up_h, up_l, found, old,
):
    width = turned.shape[0]
    classes = predictions.shape[0]
    blocks, lower, each, total = layout(width, classes)
    count = width // step
    scale = 1.0 / total_rows
    padded = found.shape[0]
    core = place[0]

    def sums(start, rows):
        part, start = divmod(start, total // 2)
        there = slice(start, start + rows)
        return jnp.where(core == part, mine[there, :], other[there, :])

    def at(k):
        return slice(k * step, (k + 1) * step)

    eye = (
        lax.broadcasted_iota(jnp.int32, (step, step), 0)
        == lax.broadcasted_iota(jnp.int32, (step, step), 1)
    ).astype(f32)
    for t, (a, b) in enumerate(pairs(blocks)):
        part = sums(t * tile, tile) * scale
        if a == b:
            part = part + ridge * eye[:tile, :tile]
        system[a * tile : (a + 1) * tile, b * tile : (b + 1) * tile] = part
        if a != b:
            system[b * tile : (b + 1) * tile, a * tile : (a + 1) * tile] = part.T
    for m in range(blocks):
        lanes = slice(m * tile, (m + 1) * tile)
        there = slice(m * tile % (width // 2), m * tile % (width // 2) + tile)
        side = core == m * tile // (width // 2)
        main, rest = 0.0, 0.0
        ends = jnp.where(side, mine_old[there, 3 * tile : 4 * tile], other_old[there, 3 * tile : 4 * tile])
        ends = ends.astype(f32).T
        first = depth_of % tile
        for i in range(3):
            lane = slice((4 + i) * tile, (5 + i) * tile)
            main = main + jnp.where(side, mine_old[there, lane], other_old[there, lane]).astype(f32)
            rest = rest + ends[first + i * (classes - tile) : first + (i + 1) * (classes - tile)]
        old[:tile, lanes] = main.T
        old[tile:, lanes] = jnp.zeros((padded - tile, tile), f32)
        old[tile:classes, lanes] = rest
        system[width:, lanes] = sums(lower + m * each, padded) * scale - old[:, lanes]
    parts = []
    for k in range(count):
        source = system if k == 0 else work
        x = split(inverse(source[at(k), at(k)], eye))
        inv_h[at(k), :], inv_l[at(k), :] = x
        column = product(split(source[(k + 1) * step :, at(k)]), x)
        parts.append(column[-padded:])
        if k == count - 1:
            break
        after = slice((k + 1) * step, width)
        column = split(column)
        low_h[after, at(k)], low_l[after, at(k)] = column[0][:-padded], column[1][:-padded]
        row = split(source[at(k), after])
        up_h[at(k), after], up_l[at(k), after] = row
        work[(k + 1) * step :, after] = source[(k + 1) * step :, after] - product(column, row)

    def backward(parts):
        for k in reversed(range(1, count)):
            before = slice(0, k * step)
            less = product(split(parts[k]), (low_h[at(k), before], low_l[at(k), before]))
            for i in range(k):
                parts[i] = parts[i] - less[:, i * step : (i + 1) * step]
        return parts

    def apply(parts):
        for k in range(count):
            now = parts[k] = product(split(parts[k]), (inv_h[at(k), :], inv_l[at(k), :]))
            if k < count - 1:
                after = slice((k + 1) * step, width)
                less = product(split(now), (up_h[at(k), after], up_l[at(k), after]))
                for i in range(k + 1, count):
                    parts[i] = parts[i] - less[:, (i - k - 1) * step : (i - k) * step]
        return backward(parts)

    for k, part in enumerate(backward(parts)):
        found[:, at(k)] = part

    def refine(state):
        short = system[width:, :] - lax.dot_general(
            found[...], system[:width, :], NN, precision=lax.Precision.HIGHEST,
            preferred_element_type=f32,
        )
        moved, size = 0.0, 0.0
        for k, part in enumerate(apply([short[:, at(k)] for k in range(count)])):
            found[:, at(k)] += part
            moved = jnp.maximum(moved, jnp.max(jnp.abs(part)))
            size = jnp.maximum(size, jnp.max(jnp.abs(found[:, at(k)])))
        return state[0] + 1, moved > 3e-4 * size

    lax.while_loop(lambda state: state[1] & (state[0] < 5), refine, (0, True))
    change = found[...]
    added = dot(change.astype(bf16), turned[...])
    updated[...] = predictions[...] + added[:classes]
    at_row = lax.broadcasted_iota(jnp.int32, (2 * tile, 2 * tile), 0)
    at_lane = lax.broadcasted_iota(jnp.int32, (2 * tile, 2 * tile), 1)
    goal = (at_row % tile) // own_width * (2 * own_width) + at_row // tile * own_width + at_row % own_width
    order = (goal == at_lane).astype(bf16)
    for u in range(width // (2 * tile)):
        one, two = slice(u * tile, (u + 1) * tile), slice(width // 2 + u * tile, width // 2 + (u + 1) * tile)
        part = jnp.concatenate([found[:, one] + old[:, one], found[:, two] + old[:, two]], axis=1)
        high, low = split(part)
        last = (part - high.astype(f32) - low.astype(f32)).astype(bf16)
        moved = (dot(high, order) + dot(low, order)) + dot(last, order)
        coeffs[:, 2 * u * tile : 2 * (u + 1) * tile] = moved[:classes]


def solve(place, mine, other, mine_old, other_old, turned, predictions, total_rows):
    width, (classes, rows) = turned.shape[0], predictions.shape
    here = pl.BlockSpec(memory_space=pltpu.VMEM)
    padded = -(-classes // 16) * 16
    return pl.pallas_call(
        functools.partial(solve_kernel, float(total_rows)),
        out_shape=(
            jax.ShapeDtypeStruct((classes, width), f32),
            jax.ShapeDtypeStruct((classes, rows), f32),
        ),
        in_specs=[pl.BlockSpec(memory_space=pltpu.SMEM)] + [here] * 6,
        out_specs=(here, here),
        scratch_shapes=[
            pltpu.VMEM((width + padded, width), f32),
            pltpu.VMEM((width + padded, width), f32),
            pltpu.VMEM((width, step), bf16),
            pltpu.VMEM((width, step), bf16),
            pltpu.VMEM((width, width), bf16),
            pltpu.VMEM((width, width), bf16),
            pltpu.VMEM((width, width), bf16),
            pltpu.VMEM((width, width), bf16),
            pltpu.VMEM((padded, width), f32),
            pltpu.VMEM((padded, width), f32),
        ],
        compiler_params=pltpu.CompilerParams(vmem_limit_bytes=48 * 1024 * 1024),
        name="solve",
    )(place, mine, other, mine_old, other_old, turned, predictions)


def exchange(x, axes):
    return lax.all_to_all(x, axes, 0, 0, tiled=True)


def gather(x, axes):
    return exchange(jnp.broadcast_to(x[None], (lax.axis_size(axes), *x.shape)), axes)


def swap(x):
    return lax.ppermute(x, "core", [(0, 1), (1, 0)])


def local(frames, freqs, phase, labels, predictions, coeffs_old):
    rows, classes = predictions.shape
    depth, own = freqs.shape
    width = phase.shape[0]
    cores = lax.axis_size("core")
    devices = width // own
    place = lax.axis_index("core").astype(jnp.int32)[None]
    first = lax.reduce_precision(coeffs_old, 8, 7)
    second = lax.reduce_precision(coeffs_old - first, 8, 7)
    olds = [part.astype(bf16) for part in (first, second, coeffs_old - first - second)]
    ends = jnp.concatenate([freqs.T] + [part[:, tile:] for part in olds], axis=1)
    ends = jnp.pad(ends, ((0, 0), (0, -ends.shape[1] % tile)))
    sent = jnp.concatenate([ends] + [part[:, :tile] for part in olds], axis=1)
    mine_sent = gather(sent, "z").reshape(-1, sent.shape[1])
    mine_sent = gather(mine_sent, ("x", "y")).reshape(width // cores, sent.shape[1])
    other_sent = swap(mine_sent)
    phase = phase.reshape(devices // cores, cores, own).swapaxes(0, 1).reshape(width, 1)
    turned, keep, send = moments(
        place, mine_sent, other_sent, frames.T, phase, labels[None, :], predictions.T
    )
    sums = (keep + swap(send)).reshape(lax.axis_size(("x", "y")), -1, tile)
    sums = exchange(sums, ("x", "y")).sum(0)
    sums = exchange(sums.reshape(lax.axis_size("z"), -1, tile), "z").sum(0)
    sums = gather(sums, "z").reshape(-1, tile)
    mine = gather(sums, ("x", "y")).reshape(-1, tile)
    other = swap(mine)
    coeffs_new, new_predictions = solve(
        place, mine, other, mine_sent, other_sent, turned, predictions.T, rows * devices
    )
    return new_predictions.T, coeffs_new.T


def solution(mesh):
    chips = mesh.devices.reshape(4, 4, 8, 2)
    inner = Mesh(chips, ("x", "y", "z", "core"))
    every = ("x", "y", "z", "core")
    placed = (P(every, None), P(None, every), P(), P(every), P(every, None), P(every, None))
    return jax.shard_map(
        local, mesh=inner, in_specs=placed, out_specs=(P(every, None), P()), check_vma=False
    )
```

```python
import functools

import jax
import jax.numpy as jnp
import numpy as np
from jax import lax
from jax.experimental import pallas as pl
from jax.experimental.pallas import tpu as pltpu
from jax.sharding import Mesh, PartitionSpec as P

f32 = jnp.float32
bf16 = jnp.bfloat16
root_two = 1.4142135623730951
ridge = 1.0
tile = 128
step = 256
own_width = 4
depth_of = 440
NN = (((1,), (0,)), ((), ()))
NT = (((1,), (1,)), ((), ()))


def cosine_coefficients(degree):
    nodes = 0.125 * np.cos(np.pi * (np.arange(400) + 0.5) / 400) + 0.125
    wanted = root_two * np.cos(2 * np.pi * np.sqrt(nodes))
    fitted = np.polynomial.chebyshev.Chebyshev.fit(nodes, wanted, degree, domain=[0, 0.25])
    return [float(c) for c in fitted.convert(kind=np.polynomial.Polynomial).coef]


cosine = cosine_coefficients(6)


def features_of(angles):
    turns = angles * (0.5 / np.pi)
    part = turns - jnp.round(turns)
    square = part * part
    value = cosine[-1] * square + cosine[-2]
    for coefficient in cosine[-3::-1]:
        value = value * square + coefficient
    return value.astype(bf16)


def dot(a, b, dims=NN):
    return lax.dot_general(a, b, dims, preferred_element_type=f32)


def split(x):
    high = x.astype(bf16)
    return high, (x - high.astype(f32)).astype(bf16)


def product(a, b):
    return dot(a[0], b[0]) + (dot(a[0], b[1]) + dot(a[1], b[0]))


def whole(x):
    return (x,)


def exact_product(a, b):
    return lax.dot_general(a[0], b[0], NN, precision=lax.Precision.HIGHEST, preferred_element_type=f32)


def store(refs, rows, lanes, parts):
    for ref, part in zip(refs, parts):
        ref[rows, lanes] = part


def load(refs, rows, lanes):
    return tuple(ref[rows, lanes] for ref in refs)


def pairs(blocks):
    return [(a, b) for a in range(blocks) for b in range(a)]


def layout(width, classes):
    blocks = width // tile
    below = len(pairs(blocks)) * tile
    lower = below + blocks // 2 * tile
    each = -(-(classes + 1) // 16) * 16
    return blocks, below, lower, each, lower + blocks * each


def coordinates(side):
    return tuple(lax.broadcasted_iota(jnp.int32, (side, side), axis) for axis in (0, 1))


def moment_kernel(
    place, mine, other, frames, phase, labels, predictions, turned, keep, send,
    packed, residual, sems,
):
    width, (classes, rows) = phase.shape[0], predictions.shape
    depth = frames.shape[0]
    blocks, below, lower, each, total = layout(width, classes)
    half = total // 2
    core = place[0]
    at_row, at_lane = coordinates(tile)
    residual[...] = jnp.zeros_like(residual)
    onehot = labels[...] == lax.broadcasted_iota(jnp.int32, (classes, rows), 0)
    residual[:classes, :] = onehot.astype(f32) - predictions[...]
    wanted = residual[...].astype(bf16)
    row = 0
    for i in range(width // step):
        here = slice(i * step, (i + 1) * step)
        first = (i * step) % (width // 2)
        side = core == (i * step) // (width // 2)
        there = slice(first, first + step)
        freqs = jnp.where(side, mine[there, :depth], other[there, :depth])
        angles = dot(freqs, frames[...]) + phase[here, :]
        block = features_of(angles)
        turned[here, :] = block
        gram = dot(block, turned[: (i + 1) * step, :], NT)
        cross = dot(wanted, block, NT)
        for j in range(step // tile):
            a = i * (step // tile) + j
            for b in range(a):
                packed[row // half, row % half : row % half + tile, :] = gram[
                    j * tile : (j + 1) * tile, b * tile : (b + 1) * tile
                ]
                row += tile
            start = lower + a * each - half
            packed[1, start : start + each, :] = cross[:, j * tile : (j + 1) * tile]
        even = gram[:tile, 2 * i * tile : (2 * i + 1) * tile]
        odd = gram[tile:, (2 * i + 1) * tile :]
        start = below + i * tile
        packed[start // half, start % half : start % half + tile, :] = jnp.where(at_row >= at_lane, even, odd)
        start = lower + (2 * i + 1) * each + classes - half
        packed[1, start : start + 1, :] = jnp.sum(jnp.where(at_row == at_lane, odd, 0.0), axis=0, keepdims=True)
    copies = [
        pltpu.make_async_copy(packed.at[core], keep, sems.at[0]),
        pltpu.make_async_copy(packed.at[1 - core], send, sems.at[1]),
    ]
    for copy in copies:
        copy.start()
    for copy in copies:
        copy.wait()


def moments(place, mine, other, frames, phase, labels, predictions):
    width, (classes, rows) = phase.shape[0], predictions.shape
    _, _, _, each, total = layout(width, classes)
    here = pl.BlockSpec(memory_space=pltpu.VMEM)
    half = jax.ShapeDtypeStruct((total // 2, tile), f32)
    return pl.pallas_call(
        moment_kernel,
        out_shape=(jax.ShapeDtypeStruct((width, rows), bf16), half, half),
        in_specs=[pl.BlockSpec(memory_space=pltpu.SMEM)] + [here] * 6,
        out_specs=(here, pl.BlockSpec(memory_space=pl.ANY), pl.BlockSpec(memory_space=pl.ANY)),
        scratch_shapes=[
            pltpu.VMEM((2, total // 2, tile), f32),
            pltpu.VMEM((each, rows), f32),
            pltpu.SemaphoreType.DMA((2,)),
        ],
        compiler_params=pltpu.CompilerParams(vmem_limit_bytes=40 * 1024 * 1024),
        name="moments",
    )(place, mine, other, frames, phase, labels, predictions)


def inverse(a, eye, bound, steps, split, product):
    scale = 2.0 / (2.0 * ridge + bound)
    spread = bound / (2.0 * ridge + bound)
    rest = eye - scale * a
    x = scale * eye
    for k in range(steps):
        gain = 2.0 / (2.0 - spread * spread)
        parts = split(rest)
        spread = spread * spread / (2.0 - spread * spread)
        x = gain * (x + (scale * rest if k == 0 else product(split(x), parts)))
        if k < steps - 1:
            rest = gain * product(parts, parts) - spread * eye
    missing = eye - product(split(a), split(x))
    return x + product(split(x), split(missing))


def solve_kernel(
    total_rows, place, mine, other, mine_old, other_old, turned, predictions, coeffs, updated,
    system, work, inv_h, inv_l, low_h, low_l, up_h, up_l, inv_e, low_e, up_e, found, old,
):
    width = turned.shape[0]
    classes = predictions.shape[0]
    blocks, below, lower, each, total = layout(width, classes)
    count = width // step
    scale = 1.0 / total_rows
    padded = found.shape[0]
    core = place[0]

    def sums(start, rows):
        part, start = divmod(start, total // 2)
        there = slice(start, start + rows)
        return jnp.where(core == part, mine[there, :], other[there, :])

    def at(k):
        return slice(k * step, (k + 1) * step)

    eye = functools.reduce(jnp.equal, coordinates(step)).astype(f32)
    at_row, at_lane = coordinates(tile)
    for t, (a, b) in enumerate(pairs(blocks)):
        part = sums(t * tile, tile) * scale
        system[a * tile : (a + 1) * tile, b * tile : (b + 1) * tile] = part
        system[b * tile : (b + 1) * tile, a * tile : (a + 1) * tile] = part.T
    for i in range(blocks // 2):
        part = sums(below + i * tile, tile)
        other_way = part.T
        diagonal = sums(lower + (2 * i + 1) * each + classes, 1)
        even = jnp.where(at_row >= at_lane, part, other_way)
        odd = jnp.where(at_row == at_lane, diagonal, jnp.where(at_row < at_lane, part, other_way))
        for a, part in ((2 * i, even), (2 * i + 1, odd)):
            there = slice(a * tile, (a + 1) * tile)
            system[there, there] = part * scale + ridge * eye[:tile, :tile]
    for m in range(blocks):
        lanes = slice(m * tile, (m + 1) * tile)
        there = slice(m * tile % (width // 2), m * tile % (width // 2) + tile)
        side = core == m * tile // (width // 2)
        main, rest = 0.0, 0.0
        ends = jnp.where(side, mine_old[there, 3 * tile : 4 * tile], other_old[there, 3 * tile : 4 * tile])
        ends = ends.astype(f32).T
        first = depth_of % tile
        for i in range(3):
            lane = slice((4 + i) * tile, (5 + i) * tile)
            main = main + jnp.where(side, mine_old[there, lane], other_old[there, lane]).astype(f32)
            rest = rest + ends[first + i * (classes - tile) : first + (i + 1) * (classes - tile)]
        old[:tile, lanes] = main.T
        old[tile:, lanes] = jnp.zeros((padded - tile, tile), f32)
        old[tile:classes, lanes] = rest
        valid = lax.broadcasted_iota(jnp.int32, (padded, tile), 0) < classes
        system[width:, lanes] = jnp.where(valid, sums(lower + m * each, padded) * scale - old[:, lanes], 0.0)
    everything = slice(0, step)

    def attempt(split, product, inv, low, up, most):
        parts = []
        for k in range(count):
            source = system if k == 0 else work
            block = source[at(k), at(k)]

            def invert(bound, steps):
                store(inv, at(k), everything, split(inverse(block, eye, bound, steps, split, product)))

            if k == 0:
                invert(2.0 * step, 7)
            else:
                small = jnp.max(jnp.sum(jnp.abs(block - ridge * eye), axis=0)) <= 6.0
                pl.when(small)(functools.partial(invert, 6.0, 3))
                pl.when(jnp.logical_not(small))(functools.partial(invert, 2.0 * step, 7))
            column = product(split(source[(k + 1) * step :, at(k)]), load(inv, at(k), everything))
            parts.append(column[-padded:])
            if k == count - 1:
                break
            after = slice((k + 1) * step, width)
            column = split(column)
            store(low, after, at(k), [part[:-padded] for part in column])
            row = split(source[at(k), after])
            store(up, at(k), after, row)
            work[(k + 1) * step :, after] = source[(k + 1) * step :, after] - product(column, row)

        def backward(parts):
            for k in reversed(range(1, count)):
                before = slice(0, k * step)
                less = product(split(parts[k]), load(low, at(k), before))
                for i in range(k):
                    parts[i] = parts[i] - less[:, i * step : (i + 1) * step]
            return parts

        def apply(parts):
            for k in range(count):
                now = parts[k] = product(split(parts[k]), load(inv, at(k), everything))
                if k < count - 1:
                    after = slice((k + 1) * step, width)
                    less = product(split(now), load(up, at(k), after))
                    for i in range(k + 1, count):
                        parts[i] = parts[i] - less[:, (i - k - 1) * step : (i - k) * step]
            return backward(parts)

        for k, part in enumerate(backward(parts)):
            found[:, at(k)] = part

        def refine(state):
            short = system[width:, :] - exact_product((found[...],), (system[:width, :],))
            moved, size = 0.0, 0.0
            for k, part in enumerate(apply([short[:, at(k)] for k in range(count)])):
                found[:, at(k)] += part
                moved = jnp.maximum(moved, jnp.max(jnp.abs(part)))
                size = jnp.maximum(size, jnp.max(jnp.abs(found[:, at(k)])))
            return state[0] + 1, moved > 1e-3 * size

        return lax.while_loop(lambda state: state[1] & (state[0] < most), refine, (0, True))[1]

    rough = attempt(split, product, (inv_h, inv_l), (low_h, low_l), (up_h, up_l), 3)

    @pl.when(rough)
    def _():
        attempt(whole, exact_product, (inv_e,), (low_e,), (up_e,), 6)

    change = found[...]
    added = dot(change.astype(bf16), turned[...])
    updated[...] = predictions[...] + added[:classes]
    at_row = lax.broadcasted_iota(jnp.int32, (2 * tile, 2 * tile), 0)
    at_lane = lax.broadcasted_iota(jnp.int32, (2 * tile, 2 * tile), 1)
    goal = (at_row % tile) // own_width * (2 * own_width) + at_row // tile * own_width + at_row % own_width
    order = (goal == at_lane).astype(bf16)
    for u in range(width // (2 * tile)):
        one, two = slice(u * tile, (u + 1) * tile), slice(width // 2 + u * tile, width // 2 + (u + 1) * tile)
        part = jnp.concatenate([found[:, one] + old[:, one], found[:, two] + old[:, two]], axis=1)
        high, low = split(part)
        last = (part - high.astype(f32) - low.astype(f32)).astype(bf16)
        moved = (dot(high, order) + dot(low, order)) + dot(last, order)
        coeffs[:, 2 * u * tile : 2 * (u + 1) * tile] = moved[:classes]


def solve(place, mine, other, mine_old, other_old, turned, predictions, total_rows):
    width, (classes, rows) = turned.shape[0], predictions.shape
    here = pl.BlockSpec(memory_space=pltpu.VMEM)
    padded = -(-classes // 16) * 16
    return pl.pallas_call(
        functools.partial(solve_kernel, float(total_rows)),
        out_shape=(
            jax.ShapeDtypeStruct((classes, width), f32),
            jax.ShapeDtypeStruct((classes, rows), f32),
        ),
        in_specs=[pl.BlockSpec(memory_space=pltpu.SMEM)] + [here] * 6,
        out_specs=(here, here),
        scratch_shapes=[
            pltpu.VMEM((width + padded, width), f32),
            pltpu.VMEM((width + padded, width), f32),
            pltpu.VMEM((width, step), bf16),
            pltpu.VMEM((width, step), bf16),
            pltpu.VMEM((width, width), bf16),
            pltpu.VMEM((width, width), bf16),
            pltpu.VMEM((width, width), bf16),
            pltpu.VMEM((width, width), bf16),
            pltpu.VMEM((width, step), f32),
            pltpu.VMEM((width, width), f32),
            pltpu.VMEM((width, width), f32),
            pltpu.VMEM((padded, width), f32),
            pltpu.VMEM((padded, width), f32),
        ],
        compiler_params=pltpu.CompilerParams(vmem_limit_bytes=48 * 1024 * 1024),
        name="solve",
    )(place, mine, other, mine_old, other_old, turned, predictions)


def exchange(x, axes):
    return lax.all_to_all(x, axes, 0, 0, tiled=True)


def gather(x, axes):
    return exchange(jnp.broadcast_to(x[None], (lax.axis_size(axes), *x.shape)), axes)


def swap(x):
    return lax.ppermute(x, "core", [(0, 1), (1, 0)])


def local(frames, freqs, phase, labels, predictions, coeffs_old):
    rows, classes = predictions.shape
    depth, own = freqs.shape
    width = phase.shape[0]
    cores = lax.axis_size("core")
    devices = width // own
    place = lax.axis_index("core").astype(jnp.int32)[None]
    first = lax.reduce_precision(coeffs_old, 8, 7)
    second = lax.reduce_precision(coeffs_old - first, 8, 7)
    olds = [part.astype(bf16) for part in (first, second, coeffs_old - first - second)]
    ends = jnp.concatenate([freqs.T] + [part[:, tile:] for part in olds], axis=1)
    ends = jnp.pad(ends, ((0, 0), (0, -ends.shape[1] % tile)))
    sent = jnp.concatenate([ends] + [part[:, :tile] for part in olds], axis=1)
    mine_sent = gather(sent, "z").reshape(-1, sent.shape[1])
    mine_sent = gather(mine_sent, ("x", "y")).reshape(width // cores, sent.shape[1])
    other_sent = swap(mine_sent)
    phase = phase.reshape(devices // cores, cores, own).swapaxes(0, 1).reshape(width, 1)
    turned, keep, send = moments(
        place, mine_sent, other_sent, frames.T, phase, labels[None, :], predictions.T
    )
    shares = lax.axis_size("z")
    sums = (keep + swap(send)).reshape(lax.axis_size(("x", "y")), -1, tile)
    sums = exchange(sums, ("x", "y")).sum(0)
    share = sums.shape[0]
    sums = jnp.pad(sums, ((0, -share % (8 * shares)), (0, 0)))
    sums = exchange(sums.reshape(shares, -1, tile), "z").sum(0)
    sums = gather(sums, "z").reshape(-1, tile)[:share]
    mine = gather(sums, ("x", "y")).reshape(-1, tile)
    other = swap(mine)
    coeffs_new, new_predictions = solve(
        place, mine, other, mine_sent, other_sent, turned, predictions.T, rows * devices
    )
    return new_predictions.T, coeffs_new.T


def solution(mesh):
    chips = mesh.devices.reshape(4, 4, 8, 2)
    inner = Mesh(chips, ("x", "y", "z", "core"))
    every = ("x", "y", "z", "core")
    placed = (P(every, None), P(None, every), P(), P(every), P(every, None), P(every, None))
    return jax.shard_map(
        local, mesh=inner, in_specs=placed, out_specs=(P(every, None), P()), check_vma=False
    )
```

```python
import functools

import jax
import jax.numpy as jnp
import numpy as np
from jax import lax
from jax.experimental import pallas as pl
from jax.experimental.pallas import tpu as pltpu
from jax.sharding import Mesh, PartitionSpec as P

f32 = jnp.float32
bf16 = jnp.bfloat16
root_two = 1.4142135623730951
ridge = 1.0
tile = 128
step = 256
own_width = 4
depth_of = 440
NN = (((1,), (0,)), ((), ()))
NT = (((1,), (1,)), ((), ()))


def cosine_coefficients(degree):
    nodes = 0.125 * np.cos(np.pi * (np.arange(400) + 0.5) / 400) + 0.125
    wanted = root_two * np.cos(2 * np.pi * np.sqrt(nodes))
    fitted = np.polynomial.chebyshev.Chebyshev.fit(nodes, wanted, degree, domain=[0, 0.25])
    return [float(c) for c in fitted.convert(kind=np.polynomial.Polynomial).coef]


cosine = cosine_coefficients(6)


def features_of(angles):
    turns = angles * (0.5 / np.pi)
    part = turns - jnp.round(turns)
    square = part * part
    value = cosine[-1] * square + cosine[-2]
    for coefficient in cosine[-3::-1]:
        value = value * square + coefficient
    return value.astype(bf16)


def dot(a, b, dims=NN):
    return lax.dot_general(a, b, dims, preferred_element_type=f32)


def split(x):
    high = x.astype(bf16)
    return high, (x - high.astype(f32)).astype(bf16)


def product(a, b):
    return dot(a[0], b[0]) + (dot(a[0], b[1]) + dot(a[1], b[0]))


def exact_product(a, b):
    return lax.dot_general(a, b, NN, precision=lax.Precision.HIGHEST, preferred_element_type=f32)


def pairs(blocks):
    return [(a, b) for a in range(blocks) for b in range(a)]


def layout(width, classes):
    blocks = width // tile
    below = len(pairs(blocks)) * tile
    lower = below + blocks // 2 * tile
    each = -(-(classes + 1) // 16) * 16
    return blocks, below, lower, each, lower + blocks * each


def coordinates(side):
    return tuple(lax.broadcasted_iota(jnp.int32, (side, side), axis) for axis in (0, 1))


def moment_kernel(
    place, mine, other, frames, phase, labels, predictions, turned, keep, send,
    packed, residual, sems,
):
    width, (classes, rows) = phase.shape[0], predictions.shape
    depth = frames.shape[0]
    blocks, below, lower, each, total = layout(width, classes)
    half = total // 2
    core = place[0]
    at_row, at_lane = coordinates(tile)
    residual[...] = jnp.zeros_like(residual)
    onehot = labels[...] == lax.broadcasted_iota(jnp.int32, (classes, rows), 0)
    residual[:classes, :] = onehot.astype(f32) - predictions[...]
    wanted = residual[...].astype(bf16)
    row = 0
    for i in range(width // step):
        here = slice(i * step, (i + 1) * step)
        first = (i * step) % (width // 2)
        side = core == (i * step) // (width // 2)
        there = slice(first, first + step)
        freqs = jnp.where(side, mine[there, :depth], other[there, :depth])
        angles = dot(freqs, frames[...]) + phase[here, :]
        block = features_of(angles)
        turned[here, :] = block
        gram = dot(block, turned[: (i + 1) * step, :], NT)
        cross = dot(wanted, block, NT)
        for j in range(step // tile):
            a = i * (step // tile) + j
            for b in range(a):
                packed[row // half, row % half : row % half + tile, :] = gram[
                    j * tile : (j + 1) * tile, b * tile : (b + 1) * tile
                ]
                row += tile
            start = lower + a * each - half
            packed[1, start : start + each, :] = cross[:, j * tile : (j + 1) * tile]
        even = gram[:tile, 2 * i * tile : (2 * i + 1) * tile]
        odd = gram[tile:, (2 * i + 1) * tile :]
        start = below + i * tile
        packed[start // half, start % half : start % half + tile, :] = jnp.where(at_row >= at_lane, even, odd)
        start = lower + (2 * i + 1) * each + classes - half
        packed[1, start : start + 1, :] = jnp.sum(jnp.where(at_row == at_lane, odd, 0.0), axis=0, keepdims=True)
    copies = [
        pltpu.make_async_copy(packed.at[core], keep, sems.at[0]),
        pltpu.make_async_copy(packed.at[1 - core], send, sems.at[1]),
    ]
    for copy in copies:
        copy.start()
    for copy in copies:
        copy.wait()


def moments(place, mine, other, frames, phase, labels, predictions):
    width, (classes, rows) = phase.shape[0], predictions.shape
    _, _, _, each, total = layout(width, classes)
    here = pl.BlockSpec(memory_space=pltpu.VMEM)
    half = jax.ShapeDtypeStruct((total // 2, tile), f32)
    return pl.pallas_call(
        moment_kernel,
        out_shape=(jax.ShapeDtypeStruct((width, rows), bf16), half, half),
        in_specs=[pl.BlockSpec(memory_space=pltpu.SMEM)] + [here] * 6,
        out_specs=(here, pl.BlockSpec(memory_space=pl.ANY), pl.BlockSpec(memory_space=pl.ANY)),
        scratch_shapes=[
            pltpu.VMEM((2, total // 2, tile), f32),
            pltpu.VMEM((each, rows), f32),
            pltpu.SemaphoreType.DMA((2,)),
        ],
        compiler_params=pltpu.CompilerParams(vmem_limit_bytes=18 * 1024 * 1024),
        name="moments",
    )(place, mine, other, frames, phase, labels, predictions)


def inverse(a, eye, bound, steps, loop=False):
    scale = 2.0 / (2.0 * ridge + bound)

    def advance(k, state):
        x, rest, spread = state
        gain = 2.0 / (2.0 - spread * spread)
        spread = spread * spread / (2.0 - spread * spread)
        parts = split(rest)
        x = gain * (x + product(split(x), parts))
        if loop or k < steps - 1:
            rest = gain * product(parts, parts) - spread * eye
        return x, rest, spread

    state = scale * eye, eye - scale * a, bound / (2.0 * ridge + bound)
    if loop:
        state = lax.fori_loop(0, steps, advance, state[:2] + (jnp.float32(state[2]),))
    else:
        x, rest, spread = state
        gain = 2.0 / (2.0 - spread * spread)
        spread = spread * spread / (2.0 - spread * spread)
        parts = split(rest)
        state = gain * (x + scale * rest), gain * product(parts, parts) - spread * eye, spread
        for k in range(1, steps):
            state = advance(k, state)
    x = state[0]
    missing = eye - product(split(a), split(x))
    return x + product(split(x), split(missing))


def solve_kernel(
    total_rows, place, mine, other, mine_old, other_old, turned, predictions, coeffs, updated,
    system, work, inv_h, inv_l, low_h, low_l, up_h, up_l, found, old,
):
    width = turned.shape[0]
    classes = predictions.shape[0]
    blocks, below, lower, each, total = layout(width, classes)
    count = width // step
    scale = 1.0 / total_rows
    padded = found.shape[0]
    core = place[0]

    def sums(start, rows):
        part, start = divmod(start, total // 2)
        there = slice(start, start + rows)
        return jnp.where(core == part, mine[there, :], other[there, :])

    def at(k):
        return slice(k * step, (k + 1) * step)

    eye = functools.reduce(jnp.equal, coordinates(step)).astype(f32)
    at_row, at_lane = coordinates(tile)
    for t, (a, b) in enumerate(pairs(blocks)):
        part = sums(t * tile, tile) * scale
        system[a * tile : (a + 1) * tile, b * tile : (b + 1) * tile] = part
        system[b * tile : (b + 1) * tile, a * tile : (a + 1) * tile] = part.T
    for i in range(blocks // 2):
        part = sums(below + i * tile, tile)
        other_way = part.T
        diagonal = sums(lower + (2 * i + 1) * each + classes, 1)
        even = jnp.where(at_row >= at_lane, part, other_way)
        odd = jnp.where(at_row == at_lane, diagonal, jnp.where(at_row < at_lane, part, other_way))
        for a, part in ((2 * i, even), (2 * i + 1, odd)):
            there = slice(a * tile, (a + 1) * tile)
            system[there, there] = part * scale + ridge * eye[:tile, :tile]
    for m in range(blocks):
        lanes = slice(m * tile, (m + 1) * tile)
        there = slice(m * tile % (width // 2), m * tile % (width // 2) + tile)
        side = core == m * tile // (width // 2)
        main, rest = 0.0, 0.0
        ends = jnp.where(side, mine_old[there, 3 * tile : 4 * tile], other_old[there, 3 * tile : 4 * tile])
        ends = ends.astype(f32).T
        first = depth_of % tile
        for i in range(3):
            lane = slice((4 + i) * tile, (5 + i) * tile)
            main = main + jnp.where(side, mine_old[there, lane], other_old[there, lane]).astype(f32)
            rest = rest + ends[first + i * (classes - tile) : first + (i + 1) * (classes - tile)]
        old[:tile, lanes] = main.T
        old[tile:, lanes] = jnp.zeros((padded - tile, tile), f32)
        old[tile:classes, lanes] = rest
        valid = lax.broadcasted_iota(jnp.int32, (padded, tile), 0) < classes
        system[width:, lanes] = jnp.where(valid, sums(lower + m * each, padded) * scale - old[:, lanes], 0.0)
    parts = []
    for k in range(count):
        source = system if k == 0 else work
        block = source[at(k), at(k)]

        def invert(bound, steps, loop=False):
            inv_h[at(k), :], inv_l[at(k), :] = split(inverse(block, eye, bound, steps, loop))

        if k == 0:
            invert(2.0 * step, 7)
        else:
            small = jnp.max(jnp.sum(jnp.abs(block - ridge * eye), axis=0)) <= 6.0
            pl.when(small)(functools.partial(invert, 6.0, 3))
            pl.when(jnp.logical_not(small))(functools.partial(invert, 2.0 * step, 7, True))
        x = inv_h[at(k), :], inv_l[at(k), :]
        column = product(split(source[(k + 1) * step :, at(k)]), x)
        parts.append(column[-padded:])
        if k == count - 1:
            break
        after = slice((k + 1) * step, width)
        column = split(column)
        low_h[after, at(k)], low_l[after, at(k)] = column[0][:-padded], column[1][:-padded]
        row = split(source[at(k), after])
        up_h[at(k), after], up_l[at(k), after] = row
        work[(k + 1) * step :, after] = source[(k + 1) * step :, after] - product(column, row)

    def backward(parts):
        for k in reversed(range(1, count)):
            before = slice(0, k * step)
            less = product(split(parts[k]), (low_h[at(k), before], low_l[at(k), before]))
            for i in range(k):
                parts[i] = parts[i] - less[:, i * step : (i + 1) * step]
        return parts

    def apply(parts):
        for k in range(count):
            now = parts[k] = product(split(parts[k]), (inv_h[at(k), :], inv_l[at(k), :]))
            if k < count - 1:
                after = slice((k + 1) * step, width)
                less = product(split(now), (up_h[at(k), after], up_l[at(k), after]))
                for i in range(k + 1, count):
                    parts[i] = parts[i] - less[:, (i - k - 1) * step : (i - k) * step]
        return backward(parts)

    for k, part in enumerate(backward(parts)):
        found[:, at(k)] = part

    def refine(state):
        short = system[width:, :] - exact_product(found[...], system[:width, :])
        moved, size = 0.0, 0.0
        for k, part in enumerate(apply([short[:, at(k)] for k in range(count)])):
            found[:, at(k)] += part
            moved += jnp.sum(part * part)
            size += jnp.sum(found[:, at(k)] * found[:, at(k)])
        return state[0] + 1, jnp.logical_not((moved <= 1e-6 * size) & (size < 1e30))

    _, rough = lax.while_loop(lambda state: state[1] & (state[0] < 3), refine, (0, True))

    @pl.when(rough)
    def _():
        found[...] = jnp.zeros_like(found)
        gained, short, ahead = (slice(i * padded, (i + 1) * padded) for i in range(3))
        tiny = 1e-30

        def norms(there):
            return jnp.sum(work[there, :] * work[there, :], axis=1, keepdims=True)

        def restart(_, carry):
            work[short, :] = system[width:, :] - exact_product(found[...], system[:width, :])
            work[ahead, :] = work[short, :]
            work[gained, :] = jnp.zeros_like(found)
            first = norms(short)

            def advance(state):
                turn, _, size = state
                image = exact_product(work[ahead, :], system[:width, :])
                far = size / jnp.maximum(jnp.sum(work[ahead, :] * image, axis=1, keepdims=True), tiny)
                work[gained, :] += far * work[ahead, :]
                work[short, :] -= far * image
                after = norms(short)
                work[ahead, :] = work[short, :] + after / jnp.maximum(size, tiny) * work[ahead, :]
                return turn + 1, jnp.max(after - 1e-12 * first) > 0.0, after

            lax.while_loop(lambda state: state[1] & (state[0] < 500), advance, (0, True, first))
            found[...] += work[gained, :]
            return carry

        lax.fori_loop(0, 3, restart, 0)

    change = found[...]
    added = dot(change.astype(bf16), turned[...])
    updated[...] = predictions[...] + added[:classes]
    at_row = lax.broadcasted_iota(jnp.int32, (2 * tile, 2 * tile), 0)
    at_lane = lax.broadcasted_iota(jnp.int32, (2 * tile, 2 * tile), 1)
    goal = (at_row % tile) // own_width * (2 * own_width) + at_row // tile * own_width + at_row % own_width
    order = (goal == at_lane).astype(bf16)
    for u in range(width // (2 * tile)):
        one, two = slice(u * tile, (u + 1) * tile), slice(width // 2 + u * tile, width // 2 + (u + 1) * tile)
        part = jnp.concatenate([found[:, one] + old[:, one], found[:, two] + old[:, two]], axis=1)
        high, low = split(part)
        last = (part - high.astype(f32) - low.astype(f32)).astype(bf16)
        moved = (dot(high, order) + dot(low, order)) + dot(last, order)
        coeffs[:, 2 * u * tile : 2 * (u + 1) * tile] = moved[:classes]


def solve(place, mine, other, mine_old, other_old, turned, predictions, total_rows):
    width, (classes, rows) = turned.shape[0], predictions.shape
    here = pl.BlockSpec(memory_space=pltpu.VMEM)
    padded = -(-classes // 16) * 16
    return pl.pallas_call(
        functools.partial(solve_kernel, float(total_rows)),
        out_shape=(
            jax.ShapeDtypeStruct((classes, width), f32),
            jax.ShapeDtypeStruct((classes, rows), f32),
        ),
        in_specs=[pl.BlockSpec(memory_space=pltpu.SMEM)] + [here] * 6,
        out_specs=(here, here),
        scratch_shapes=[
            pltpu.VMEM((width + padded, width), f32),
            pltpu.VMEM((width + padded, width), f32),
            pltpu.VMEM((width, step), bf16),
            pltpu.VMEM((width, step), bf16),
            pltpu.VMEM((width, width), bf16),
            pltpu.VMEM((width, width), bf16),
            pltpu.VMEM((width, width), bf16),
            pltpu.VMEM((width, width), bf16),
            pltpu.VMEM((padded, width), f32),
            pltpu.VMEM((padded, width), f32),
        ],
        compiler_params=pltpu.CompilerParams(vmem_limit_bytes=38 * 1024 * 1024),
        name="solve",
    )(place, mine, other, mine_old, other_old, turned, predictions)


def exchange(x, axes):
    return lax.all_to_all(x, axes, 0, 0, tiled=True)


def gather(x, axes):
    return exchange(jnp.broadcast_to(x[None], (lax.axis_size(axes), *x.shape)), axes)


def swap(x):
    return lax.ppermute(x, "core", [(0, 1), (1, 0)])


def local(frames, freqs, phase, labels, predictions, coeffs_old):
    rows, classes = predictions.shape
    depth, own = freqs.shape
    width = phase.shape[0]
    cores = lax.axis_size("core")
    devices = width // own
    place = lax.axis_index("core").astype(jnp.int32)[None]
    first = lax.reduce_precision(coeffs_old, 8, 7)
    second = lax.reduce_precision(coeffs_old - first, 8, 7)
    olds = [part.astype(bf16) for part in (first, second, coeffs_old - first - second)]
    ends = jnp.concatenate([freqs.T] + [part[:, tile:] for part in olds], axis=1)
    ends = jnp.pad(ends, ((0, 0), (0, -ends.shape[1] % tile)))
    sent = jnp.concatenate([ends] + [part[:, :tile] for part in olds], axis=1)
    mine_sent = gather(sent, "z").reshape(-1, sent.shape[1])
    mine_sent = gather(mine_sent, ("x", "y")).reshape(width // cores, sent.shape[1])
    other_sent = swap(mine_sent)
    phase = phase.reshape(devices // cores, cores, own).swapaxes(0, 1).reshape(width, 1)
    turned, keep, send = moments(
        place, mine_sent, other_sent, frames.T, phase, labels[None, :], predictions.T
    )
    shares = lax.axis_size("z")
    sums = (keep + swap(send)).reshape(lax.axis_size(("x", "y")), -1, tile)
    sums = exchange(sums, ("x", "y")).sum(0)
    share = sums.shape[0]
    sums = jnp.pad(sums, ((0, -share % (8 * shares)), (0, 0)))
    sums = exchange(sums.reshape(shares, -1, tile), "z").sum(0)
    sums = gather(sums, "z").reshape(-1, tile)[:share]
    mine = gather(sums, ("x", "y")).reshape(-1, tile)
    other = swap(mine)
    coeffs_new, new_predictions = solve(
        place, mine, other, mine_sent, other_sent, turned, predictions.T, rows * devices
    )
    return new_predictions.T, coeffs_new.T


def solution(mesh):
    chips = mesh.devices.reshape(4, 4, 8, 2)
    inner = Mesh(chips, ("x", "y", "z", "core"))
    every = ("x", "y", "z", "core")
    placed = (P(every, None), P(None, every), P(), P(every), P(every, None), P(every, None))
    return jax.shard_map(
        local, mesh=inner, in_specs=placed, out_specs=(P(every, None), P()), check_vma=False
    )
```

```python
import functools

import jax
import jax.numpy as jnp
import numpy as np
from jax import lax
from jax.experimental import pallas as pl
from jax.experimental.pallas import tpu as pltpu
from jax.sharding import Mesh, PartitionSpec as P

f32 = jnp.float32
bf16 = jnp.bfloat16
root_two = 1.4142135623730951
ridge = 1.0
tile = 128
step = 256
own_width = 4
depth_of = 440
NN = (((1,), (0,)), ((), ()))
NT = (((1,), (1,)), ((), ()))


def cosine_coefficients(degree):
    nodes = 0.125 * np.cos(np.pi * (np.arange(400) + 0.5) / 400) + 0.125
    wanted = root_two * np.cos(2 * np.pi * np.sqrt(nodes))
    fitted = np.polynomial.chebyshev.Chebyshev.fit(nodes, wanted, degree, domain=[0, 0.25])
    return [float(c) for c in fitted.convert(kind=np.polynomial.Polynomial).coef]


cosine = cosine_coefficients(6)


def features_of(angles):
    turns = angles * (0.5 / np.pi)
    part = turns - jnp.round(turns)
    square = part * part
    value = cosine[-1] * square + cosine[-2]
    for coefficient in cosine[-3::-1]:
        value = value * square + coefficient
    return value.astype(bf16)


def dot(a, b, dims=NN):
    return lax.dot_general(a, b, dims, preferred_element_type=f32)


def split(x):
    high = x.astype(bf16)
    return high, (x - high.astype(f32)).astype(bf16)


def product(a, b):
    rows = a[0].shape[0]
    both = dot(jnp.concatenate(a, axis=0), b[0])
    return both[:rows] + (both[rows:] + dot(a[0], b[1]))


def exact_product(a, b):
    return lax.dot_general(a, b, NN, precision=lax.Precision.HIGHEST, preferred_element_type=f32)


def three(x):
    high, low = split(x)
    return high, low, (x - high.astype(f32) - low.astype(f32)).astype(bf16)


def wide_product(x, wide):
    rows, depth = x.shape
    parts = jnp.concatenate(three(x), axis=0)
    result = []
    for j in range(depth // step):
        high, low, last = three(wide[:depth, j * step : (j + 1) * step])
        one = dot(parts, high)
        two = dot(parts[: 2 * rows], low)
        small = one[2 * rows :] + two[rows:] + dot(parts[:rows], last)
        result.append(one[:rows] + ((one[rows : 2 * rows] + two[:rows]) + small))
    return jnp.concatenate(result, axis=1)


def layout(width, classes):
    each = -(-(classes + 1) // 16) * 16
    places, ends, rows = {}, [], [0, 0]
    for a in range(0, width // tile, 2):
        blocks = [(c, b) for c in (a, a + 1) for b in range(c)] + [(a, a)]
        for n, block in enumerate(blocks):
            places[block] = (n % 2, rows[n % 2])
            rows[n % 2] += tile
        for part in range(2):
            places["cross", a + part] = (part, rows[part])
            rows[part] += each
        ends.append(rows[0])
    return each, places, ends


def coordinates(side):
    return tuple(lax.broadcasted_iota(jnp.int32, (side, side), axis) for axis in (0, 1))


def moment_kernel(
    place, mine, other, frames, phase, labels, predictions, turned, keep, send,
    packed, residual, sems,
):
    width, (classes, rows) = phase.shape[0], predictions.shape
    depth = frames.shape[0]
    each, places, ends = layout(width, classes)
    core = place[0]
    at_row, at_lane = coordinates(tile)
    copies = []

    def put(name, value, behind=0):
        part, row = places[name]
        packed[part, row + behind : row + behind + value.shape[0], :] = value

    residual[...] = jnp.zeros_like(residual)
    onehot = labels[...] == lax.broadcasted_iota(jnp.int32, (classes, rows), 0)
    residual[:classes, :] = onehot.astype(f32) - predictions[...]
    wanted = residual[...].astype(bf16)
    for i in range(width // step):
        here = slice(i * step, (i + 1) * step)
        first = (i * step) % (width // 2)
        side = core == (i * step) // (width // 2)
        there = slice(first, first + step)
        freqs = jnp.where(side, mine[there, :depth], other[there, :depth])
        angles = dot(freqs, frames[...]) + phase[here, :]
        block = features_of(angles)
        turned[here, :] = block
        gram = dot(block, turned[: (i + 1) * step, :], NT)
        cross = dot(wanted, block, NT)
        for j in range(step // tile):
            a = i * (step // tile) + j
            for b in range(a):
                put((a, b), gram[j * tile : (j + 1) * tile, b * tile : (b + 1) * tile])
            put(("cross", a), cross[:, j * tile : (j + 1) * tile])
        even = gram[:tile, 2 * i * tile : (2 * i + 1) * tile]
        odd = gram[tile:, (2 * i + 1) * tile :]
        put((2 * i, 2 * i), jnp.where(at_row >= at_lane, even, odd))
        diagonal = jnp.sum(jnp.where(at_row == at_lane, odd, 0.0), axis=0, keepdims=True)
        put(("cross", 2 * i + 1), diagonal, classes)
        start = ends[i - 1] if i else 0
        done = pl.ds(start, ends[i] - start)
        for n, target in enumerate((keep, send)):
            source = packed.at[core if n == 0 else 1 - core, done]
            copy = pltpu.make_async_copy(source, target.at[done], sems.at[i, n])
            copy.start()
            copies.append(copy)
    for copy in copies:
        copy.wait()


def moments(place, mine, other, frames, phase, labels, predictions):
    width, (classes, rows) = phase.shape[0], predictions.shape
    each, _, ends = layout(width, classes)
    here = pl.BlockSpec(memory_space=pltpu.VMEM)
    half = jax.ShapeDtypeStruct((ends[-1], tile), f32)
    return pl.pallas_call(
        moment_kernel,
        out_shape=(jax.ShapeDtypeStruct((width, rows), bf16), half, half),
        in_specs=[pl.BlockSpec(memory_space=pltpu.SMEM)] + [here] * 6,
        out_specs=(here, pl.BlockSpec(memory_space=pl.ANY), pl.BlockSpec(memory_space=pl.ANY)),
        scratch_shapes=[
            pltpu.VMEM((2, ends[-1], tile), f32),
            pltpu.VMEM((each, rows), f32),
            pltpu.SemaphoreType.DMA((len(ends), 2)),
        ],
        compiler_params=pltpu.CompilerParams(vmem_limit_bytes=18 * 1024 * 1024),
        name="moments",
    )(place, mine, other, frames, phase, labels, predictions)


def inverse(a, eye, bound, steps, loop=False):
    scale = 2.0 / (2.0 * ridge + bound)

    def advance(k, state):
        x, rest, spread = state
        gain = 2.0 / (2.0 - spread * spread)
        spread = spread * spread / (2.0 - spread * spread)
        parts = split(rest)
        x = gain * (x + product(split(x), parts))
        if loop or k < steps - 1:
            rest = gain * product(parts, parts) - spread * eye
        return x, rest, spread

    state = scale * eye, eye - scale * a, bound / (2.0 * ridge + bound)
    if loop:
        state = lax.fori_loop(0, steps, advance, state[:2] + (jnp.float32(state[2]),))
    else:
        x, rest, spread = state
        gain = 2.0 / (2.0 - spread * spread)
        spread = spread * spread / (2.0 - spread * spread)
        parts = split(rest)
        state = gain * (x + scale * rest), gain * product(parts, parts) - spread * eye, spread
        for k in range(1, steps):
            state = advance(k, state)
    x = state[0]
    missing = eye - product(split(a), split(x))
    return x + product(split(x), split(missing))


def solve_kernel(
    total_rows, place, mine, other, mine_old, other_old, turned, predictions, coeffs, updated,
    system, work, inv_h, inv_l, low_h, low_l, up_h, up_l, found, old,
):
    width = turned.shape[0]
    classes = predictions.shape[0]
    _, places, _ = layout(width, classes)
    blocks, count = width // tile, width // step
    scale = 1.0 / total_rows
    padded = found.shape[0]
    core = place[0]

    def sums(name, rows, behind=0):
        part, start = places[name]
        there = slice(start + behind, start + behind + rows)
        return jnp.where(core == part, mine[there, :], other[there, :])

    def at(k):
        return slice(k * step, (k + 1) * step)

    eye = functools.reduce(jnp.equal, coordinates(step)).astype(f32)
    at_row, at_lane = coordinates(tile)
    for a in range(blocks):
        for b in range(a):
            part = sums((a, b), tile) * scale
            system[a * tile : (a + 1) * tile, b * tile : (b + 1) * tile] = part
            system[b * tile : (b + 1) * tile, a * tile : (a + 1) * tile] = part.T
    for i in range(blocks // 2):
        part = sums((2 * i, 2 * i), tile)
        other_way = part.T
        diagonal = sums(("cross", 2 * i + 1), 1, classes)
        even = jnp.where(at_row >= at_lane, part, other_way)
        odd = jnp.where(at_row == at_lane, diagonal, jnp.where(at_row < at_lane, part, other_way))
        for a, part in ((2 * i, even), (2 * i + 1, odd)):
            there = slice(a * tile, (a + 1) * tile)
            system[there, there] = part * scale + ridge * eye[:tile, :tile]
    for m in range(blocks):
        lanes = slice(m * tile, (m + 1) * tile)
        there = slice(m * tile % (width // 2), m * tile % (width // 2) + tile)
        side = core == m * tile // (width // 2)
        main, rest = 0.0, 0.0
        ends = jnp.where(side, mine_old[there, 3 * tile : 4 * tile], other_old[there, 3 * tile : 4 * tile])
        ends = ends.astype(f32).T
        first = depth_of % tile
        for i in range(3):
            lane = slice((4 + i) * tile, (5 + i) * tile)
            main = main + jnp.where(side, mine_old[there, lane], other_old[there, lane]).astype(f32)
            rest = rest + ends[first + i * (classes - tile) : first + (i + 1) * (classes - tile)]
        old[:tile, lanes] = main.T
        old[tile:, lanes] = jnp.zeros((padded - tile, tile), f32)
        old[tile:classes, lanes] = rest
        valid = lax.broadcasted_iota(jnp.int32, (padded, tile), 0) < classes
        system[width:, lanes] = jnp.where(valid, sums(("cross", m), padded) * scale - old[:, lanes], 0.0)
    parts = []
    for k in range(count):
        source = system if k == 0 else work
        block = source[at(k), at(k)]

        def invert(bound, steps, loop=False):
            inv_h[at(k), :], inv_l[at(k), :] = split(inverse(block, eye, bound, steps, loop))

        if k == 0:
            invert(2.0 * step, 7)
        else:
            small = jnp.max(jnp.sum(jnp.abs(block - ridge * eye), axis=0)) <= 6.0
            pl.when(small)(functools.partial(invert, 6.0, 3))
            pl.when(jnp.logical_not(small))(functools.partial(invert, 2.0 * step, 7, True))
        x = inv_h[at(k), :], inv_l[at(k), :]
        column = product(split(source[(k + 1) * step :, at(k)]), x)
        parts.append(column[-padded:])
        if k == count - 1:
            break
        after = slice((k + 1) * step, width)
        column = split(column)
        low_h[after, at(k)], low_l[after, at(k)] = column[0][:-padded], column[1][:-padded]
        row = split(source[at(k), after])
        up_h[at(k), after], up_l[at(k), after] = row
        work[(k + 1) * step :, after] = source[(k + 1) * step :, after] - product(column, row)

    def backward(parts):
        for k in reversed(range(1, count)):
            before = slice(0, k * step)
            less = product(split(parts[k]), (low_h[at(k), before], low_l[at(k), before]))
            for i in range(k):
                parts[i] = parts[i] - less[:, i * step : (i + 1) * step]
        return parts

    def apply(parts):
        for k in range(count):
            now = parts[k] = product(split(parts[k]), (inv_h[at(k), :], inv_l[at(k), :]))
            if k < count - 1:
                after = slice((k + 1) * step, width)
                less = product(split(now), (up_h[at(k), after], up_l[at(k), after]))
                for i in range(k + 1, count):
                    parts[i] = parts[i] - less[:, (i - k - 1) * step : (i - k) * step]
        return backward(parts)

    for k, part in enumerate(backward(parts)):
        found[:, at(k)] = part

    def refine(state):
        short = system[width:, :] - wide_product(found[...], system)
        moved, size = 0.0, 0.0
        for k, part in enumerate(apply([short[:, at(k)] for k in range(count)])):
            found[:, at(k)] += part
            moved += jnp.sum(part * part)
            size += jnp.sum(found[:, at(k)] * found[:, at(k)])
        return state[0] + 1, jnp.logical_not((moved <= 1e-6 * size) & (size < 1e30))

    _, rough = lax.while_loop(lambda state: state[1] & (state[0] < 3), refine, (0, True))

    @pl.when(rough)
    def _():
        found[...] = jnp.zeros_like(found)
        gained, short, ahead = (slice(i * padded, (i + 1) * padded) for i in range(3))
        tiny = 1e-30

        def norms(there):
            return jnp.sum(work[there, :] * work[there, :], axis=1, keepdims=True)

        def restart(_, carry):
            work[short, :] = system[width:, :] - exact_product(found[...], system[:width, :])
            work[ahead, :] = work[short, :]
            work[gained, :] = jnp.zeros_like(found)
            first = norms(short)

            def advance(state):
                turn, _, size = state
                image = exact_product(work[ahead, :], system[:width, :])
                far = size / jnp.maximum(jnp.sum(work[ahead, :] * image, axis=1, keepdims=True), tiny)
                work[gained, :] += far * work[ahead, :]
                work[short, :] -= far * image
                after = norms(short)
                work[ahead, :] = work[short, :] + after / jnp.maximum(size, tiny) * work[ahead, :]
                return turn + 1, jnp.max(after - 1e-12 * first) > 0.0, after

            lax.while_loop(lambda state: state[1] & (state[0] < 500), advance, (0, True, first))
            found[...] += work[gained, :]
            return carry

        lax.fori_loop(0, 3, restart, 0)

    change = found[...]
    added = dot(change.astype(bf16), turned[...])
    updated[...] = predictions[...] + added[:classes]
    at_row = lax.broadcasted_iota(jnp.int32, (2 * tile, 2 * tile), 0)
    at_lane = lax.broadcasted_iota(jnp.int32, (2 * tile, 2 * tile), 1)
    goal = (at_row % tile) // own_width * (2 * own_width) + at_row // tile * own_width + at_row % own_width
    order = (goal == at_lane).astype(bf16)
    for u in range(width // (2 * tile)):
        one, two = slice(u * tile, (u + 1) * tile), slice(width // 2 + u * tile, width // 2 + (u + 1) * tile)
        part = jnp.concatenate([found[:, one] + old[:, one], found[:, two] + old[:, two]], axis=1)
        high, low, last = (dot(piece, order) for piece in three(part))
        moved = (high + low) + last
        coeffs[:, 2 * u * tile : 2 * (u + 1) * tile] = moved[:classes]


def solve(place, mine, other, mine_old, other_old, turned, predictions, total_rows):
    width, (classes, rows) = turned.shape[0], predictions.shape
    here = pl.BlockSpec(memory_space=pltpu.VMEM)
    padded = -(-classes // 16) * 16
    return pl.pallas_call(
        functools.partial(solve_kernel, float(total_rows)),
        out_shape=(
            jax.ShapeDtypeStruct((classes, width), f32),
            jax.ShapeDtypeStruct((classes, rows), f32),
        ),
        in_specs=[pl.BlockSpec(memory_space=pltpu.SMEM)] + [here] * 6,
        out_specs=(here, here),
        scratch_shapes=[
            pltpu.VMEM((width + padded, width), f32),
            pltpu.VMEM((width + padded, width), f32),
            pltpu.VMEM((width, step), bf16),
            pltpu.VMEM((width, step), bf16),
            pltpu.VMEM((width, width), bf16),
            pltpu.VMEM((width, width), bf16),
            pltpu.VMEM((width, width), bf16),
            pltpu.VMEM((width, width), bf16),
            pltpu.VMEM((padded, width), f32),
            pltpu.VMEM((padded, width), f32),
        ],
        compiler_params=pltpu.CompilerParams(vmem_limit_bytes=38 * 1024 * 1024),
        name="solve",
    )(place, mine, other, mine_old, other_old, turned, predictions)


def total_kernel(shares, result):
    used = shares.shape[1]
    result[:used, :] = functools.reduce(jnp.add, [shares[n] for n in range(shares.shape[0])])
    if used < result.shape[0]:
        result[used:, :] = jnp.zeros((result.shape[0] - used, result.shape[1]), f32)


def total(shares, rows):
    here = pl.BlockSpec(memory_space=pltpu.VMEM)
    return pl.pallas_call(
        total_kernel,
        out_shape=jax.ShapeDtypeStruct((rows, shares.shape[2]), f32),
        in_specs=[here],
        out_specs=here,
        name="total",
    )(shares)


def exchange(x, axes):
    return lax.all_to_all(x, axes, 0, 0, tiled=True)


def gather(x, axes):
    return exchange(jnp.broadcast_to(x[None], (lax.axis_size(axes), *x.shape)), axes)


def swap(x):
    return lax.ppermute(x, "core", [(0, 1), (1, 0)])


def local(frames, freqs, phase, labels, predictions, coeffs_old):
    rows, classes = predictions.shape
    depth, own = freqs.shape
    width = phase.shape[0]
    cores = lax.axis_size("core")
    devices = width // own
    place = lax.axis_index("core").astype(jnp.int32)[None]
    first = lax.reduce_precision(coeffs_old, 8, 7)
    second = lax.reduce_precision(coeffs_old - first, 8, 7)
    olds = [part.astype(bf16) for part in (first, second, coeffs_old - first - second)]
    filled = -(-(depth + 3 * (classes - tile)) // tile) * tile
    lanes = filled + 3 * tile

    def put(x, start):
        return jnp.pad(x, ((0, 0), (start, lanes - start - x.shape[1])))

    sent = put(freqs.T, 0)
    for i, part in enumerate(olds):
        sent += put(part[:, tile:], depth + i * (classes - tile)) + put(part[:, :tile], filled + i * tile)
    mine_sent = gather(sent, "z").reshape(-1, sent.shape[1])
    mine_sent = gather(mine_sent, ("x", "y")).reshape(width // cores, sent.shape[1])
    other_sent = swap(mine_sent)
    phase = phase.reshape(devices // cores, cores, own).swapaxes(0, 1).reshape(width, 1)
    turned, keep, send = moments(
        place, mine_sent, other_sent, frames.T, phase, labels[None, :], predictions.T
    )
    shares = lax.axis_size("z")
    sums = (keep + swap(send)).reshape(lax.axis_size(("x", "y")), -1, tile)
    share = sums.shape[1]
    sums = total(exchange(sums, ("x", "y")), -(-share // (8 * shares)) * 8 * shares)
    sums = exchange(sums.reshape(shares, -1, tile), "z").sum(0)
    sums = gather(sums, "z").reshape(-1, tile)[:share]
    mine = gather(sums, ("x", "y")).reshape(-1, tile)
    other = swap(mine)
    coeffs_new, new_predictions = solve(
        place, mine, other, mine_sent, other_sent, turned, predictions.T, rows * devices
    )
    return new_predictions.T, coeffs_new.T


def solution(mesh):
    chips = mesh.devices.reshape(4, 4, 8, 2)
    inner = Mesh(chips, ("x", "y", "z", "core"))
    every = ("x", "y", "z", "core")
    placed = (P(every, None), P(None, every), P(), P(every), P(every, None), P(every, None))
    return jax.shard_map(
        local, mesh=inner, in_specs=placed, out_specs=(P(every, None), P()), check_vma=False
    )
```

```python
import functools

import jax
import jax.numpy as jnp
import numpy as np
from jax import lax
from jax.experimental import pallas as pl
from jax.experimental.pallas import tpu as pltpu
from jax.sharding import Mesh, PartitionSpec as P

f32 = jnp.float32
bf16 = jnp.bfloat16
root_two = 1.4142135623730951
ridge = 1.0
tile = 128
step = 256
own_width = 4
depth_of = 440
NN = (((1,), (0,)), ((), ()))
NT = (((1,), (1,)), ((), ()))


def cosine_coefficients(degree):
    nodes = 0.125 * np.cos(np.pi * (np.arange(400) + 0.5) / 400) + 0.125
    wanted = root_two * np.cos(2 * np.pi * np.sqrt(nodes))
    fitted = np.polynomial.chebyshev.Chebyshev.fit(nodes, wanted, degree, domain=[0, 0.25])
    return [float(c) for c in fitted.convert(kind=np.polynomial.Polynomial).coef]


cosine = cosine_coefficients(6)


def features_of(angles):
    turns = angles * (0.5 / np.pi)
    part = turns - jnp.round(turns)
    square = part * part
    value = cosine[-1] * square + cosine[-2]
    for coefficient in cosine[-3::-1]:
        value = value * square + coefficient
    return value.astype(bf16)


def dot(a, b, dims=NN):
    return lax.dot_general(a, b, dims, preferred_element_type=f32)


def split(x):
    high = x.astype(bf16)
    return high, (x - high.astype(f32)).astype(bf16)


def product(a, b):
    rows = a[0].shape[0]
    both = dot(jnp.concatenate(a, axis=0), b[0])
    return both[:rows] + (both[rows:] + dot(a[0], b[1]))


def exact_product(a, b):
    return lax.dot_general(a, b, NN, precision=lax.Precision.HIGHEST, preferred_element_type=f32)


def three(x):
    high, low = split(x)
    return high, low, (x - high.astype(f32) - low.astype(f32)).astype(bf16)


def wide_product(x, wide):
    rows, depth = x.shape
    parts = jnp.concatenate(three(x), axis=0)
    result = []
    for j in range(depth // step):
        high, low, last = three(wide[:depth, j * step : (j + 1) * step])
        one = dot(parts, high)
        two = dot(parts[: 2 * rows], low)
        small = one[2 * rows :] + two[rows:] + dot(parts[:rows], last)
        result.append(one[:rows] + ((one[rows : 2 * rows] + two[:rows]) + small))
    return jnp.concatenate(result, axis=1)


def pairs(blocks):
    return [(a, b) for a in range(blocks) for b in range(a)]


def layout(width, classes):
    blocks = width // tile
    below = len(pairs(blocks)) * tile
    lower = below + blocks // 2 * tile
    each = -(-(classes + 1) // 16) * 16
    return blocks, below, lower, each, lower + blocks * each


def coordinates(side):
    return tuple(lax.broadcasted_iota(jnp.int32, (side, side), axis) for axis in (0, 1))


def moment_kernel(
    place, mine, other, frames, phase, labels, predictions, turned, packed, residual,
):
    width, (classes, rows) = phase.shape[0], predictions.shape
    depth = frames.shape[0]
    blocks, below, lower, each, total = layout(width, classes)
    half = total // 2
    core = place[0]
    part_of = (core, 1 - core)
    at_row, at_lane = coordinates(tile)
    residual[...] = jnp.zeros_like(residual)
    onehot = labels[...] == lax.broadcasted_iota(jnp.int32, (classes, rows), 0)
    residual[:classes, :] = onehot.astype(f32) - predictions[...]
    wanted = residual[...].astype(bf16)
    row = 0
    for i in range(width // step):
        here = slice(i * step, (i + 1) * step)
        first = (i * step) % (width // 2)
        side = core == (i * step) // (width // 2)
        there = slice(first, first + step)
        freqs = jnp.where(side, mine[there, :depth], other[there, :depth])
        angles = dot(freqs, frames[...]) + phase[here, :]
        block = features_of(angles)
        turned[here, :] = block
        gram = dot(block, turned[: (i + 1) * step, :], NT)
        cross = dot(wanted, block, NT)
        for j in range(step // tile):
            a = i * (step // tile) + j
            for b in range(a):
                packed[part_of[row // half], row % half : row % half + tile, :] = gram[
                    j * tile : (j + 1) * tile, b * tile : (b + 1) * tile
                ]
                row += tile
            start = lower + a * each - half
            packed[part_of[1], start : start + each, :] = cross[:, j * tile : (j + 1) * tile]
        even = gram[:tile, 2 * i * tile : (2 * i + 1) * tile]
        odd = gram[tile:, (2 * i + 1) * tile :]
        start = below + i * tile
        packed[part_of[start // half], start % half : start % half + tile, :] = jnp.where(at_row >= at_lane, even, odd)
        start = lower + (2 * i + 1) * each + classes - half
        packed[part_of[1], start : start + 1, :] = jnp.sum(jnp.where(at_row == at_lane, odd, 0.0), axis=0, keepdims=True)


def moments(place, mine, other, frames, phase, labels, predictions):
    width, (classes, rows) = phase.shape[0], predictions.shape
    _, _, _, each, total = layout(width, classes)
    here = pl.BlockSpec(memory_space=pltpu.VMEM)
    return pl.pallas_call(
        moment_kernel,
        out_shape=(
            jax.ShapeDtypeStruct((width, rows), bf16),
            jax.ShapeDtypeStruct((2, total // 2, tile), f32),
        ),
        in_specs=[pl.BlockSpec(memory_space=pltpu.SMEM)] + [here] * 6,
        out_specs=(here, here),
        scratch_shapes=[pltpu.VMEM((each, rows), f32)],
        compiler_params=pltpu.CompilerParams(vmem_limit_bytes=20 * 1024 * 1024),
        name="moments",
    )(place, mine, other, frames, phase, labels, predictions)


def inverse(a, eye, bound, steps, loop=False, correct=True):
    scale = 2.0 / (2.0 * ridge + bound)

    def advance(k, state):
        x, rest, spread = state
        gain = 2.0 / (2.0 - spread * spread)
        spread = spread * spread / (2.0 - spread * spread)
        parts = split(rest)
        x = gain * (x + product(split(x), parts))
        if loop or k < steps - 1:
            rest = gain * product(parts, parts) - spread * eye
        return x, rest, spread

    state = scale * eye, eye - scale * a, bound / (2.0 * ridge + bound)
    if loop:
        state = lax.fori_loop(0, steps, advance, state[:2] + (jnp.float32(state[2]),))
    else:
        x, rest, spread = state
        gain = 2.0 / (2.0 - spread * spread)
        spread = spread * spread / (2.0 - spread * spread)
        parts = split(rest)
        state = gain * (x + scale * rest), gain * product(parts, parts) - spread * eye, spread
        for k in range(1, steps):
            state = advance(k, state)
    x = state[0]
    if not correct:
        return x
    missing = eye - product(split(a), split(x))
    return x + product(split(x), split(missing))


def solve_kernel(
    total_rows, place, mine, other, mine_old, other_old, turned, predictions, coeffs, updated,
    system, work, inv_h, inv_l, low_h, low_l, up_h, up_l, found, old,
):
    width = turned.shape[0]
    classes = predictions.shape[0]
    blocks, below, lower, each, total = layout(width, classes)
    count = width // step
    scale = 1.0 / total_rows
    padded = found.shape[0]
    core = place[0]

    def sums(start, rows):
        part, start = divmod(start, total // 2)
        there = slice(start, start + rows)
        return jnp.where(core == part, mine[there, :], other[there, :])

    def at(k):
        return slice(k * step, (k + 1) * step)

    eye = functools.reduce(jnp.equal, coordinates(step)).astype(f32)
    at_row, at_lane = coordinates(tile)
    for t, (a, b) in enumerate(pairs(blocks)):
        part = sums(t * tile, tile) * scale
        system[a * tile : (a + 1) * tile, b * tile : (b + 1) * tile] = part
        system[b * tile : (b + 1) * tile, a * tile : (a + 1) * tile] = part.T
    for i in range(blocks // 2):
        part = sums(below + i * tile, tile)
        other_way = part.T
        diagonal = sums(lower + (2 * i + 1) * each + classes, 1)
        even = jnp.where(at_row >= at_lane, part, other_way)
        odd = jnp.where(at_row == at_lane, diagonal, jnp.where(at_row < at_lane, part, other_way))
        for a, part in ((2 * i, even), (2 * i + 1, odd)):
            there = slice(a * tile, (a + 1) * tile)
            system[there, there] = part * scale + ridge * eye[:tile, :tile]
    for m in range(blocks):
        lanes = slice(m * tile, (m + 1) * tile)
        there = slice(m * tile % (width // 2), m * tile % (width // 2) + tile)
        side = core == m * tile // (width // 2)
        main, rest = 0.0, 0.0
        ends = jnp.where(side, mine_old[there, 3 * tile : 4 * tile], other_old[there, 3 * tile : 4 * tile])
        ends = ends.astype(f32).T
        first = depth_of % tile
        for i in range(3):
            lane = slice((4 + i) * tile, (5 + i) * tile)
            main = main + jnp.where(side, mine_old[there, lane], other_old[there, lane]).astype(f32)
            rest = rest + ends[first + i * (classes - tile) : first + (i + 1) * (classes - tile)]
        old[:tile, lanes] = main.T
        old[tile:, lanes] = jnp.zeros((padded - tile, tile), f32)
        old[tile:classes, lanes] = rest
        valid = lax.broadcasted_iota(jnp.int32, (padded, tile), 0) < classes
        system[width:, lanes] = jnp.where(valid, sums(lower + m * each, padded) * scale - old[:, lanes], 0.0)
    parts = []
    for k in range(count):
        source = system if k == 0 else work
        block = source[at(k), at(k)]

        def invert(bound, steps, **options):
            inv_h[at(k), :], inv_l[at(k), :] = split(inverse(block, eye, bound, steps, **options))

        if k == 0:
            invert(2.0 * step, 7)
        else:
            small = jnp.max(jnp.sum(jnp.abs(block - ridge * eye), axis=0)) <= 6.0
            pl.when(small)(functools.partial(invert, 6.0, 4, correct=False))
            pl.when(jnp.logical_not(small))(functools.partial(invert, 2.0 * step, 7, loop=True))
        x = inv_h[at(k), :], inv_l[at(k), :]
        column = product(split(source[(k + 1) * step :, at(k)]), x)
        parts.append(column[-padded:])
        if k == count - 1:
            break
        after = slice((k + 1) * step, width)
        column = split(column)
        low_h[after, at(k)], low_l[after, at(k)] = column[0][:-padded], column[1][:-padded]
        row = split(source[at(k), after])
        up_h[at(k), after], up_l[at(k), after] = row
        work[(k + 1) * step :, after] = source[(k + 1) * step :, after] - product(column, row)

    def backward(parts):
        for k in reversed(range(1, count)):
            before = slice(0, k * step)
            less = product(split(parts[k]), (low_h[at(k), before], low_l[at(k), before]))
            for i in range(k):
                parts[i] = parts[i] - less[:, i * step : (i + 1) * step]
        return parts

    def apply(parts):
        for k in range(count):
            now = parts[k] = product(split(parts[k]), (inv_h[at(k), :], inv_l[at(k), :]))
            if k < count - 1:
                after = slice((k + 1) * step, width)
                less = product(split(now), (up_h[at(k), after], up_l[at(k), after]))
                for i in range(k + 1, count):
                    parts[i] = parts[i] - less[:, (i - k - 1) * step : (i - k) * step]
        return backward(parts)

    for k, part in enumerate(backward(parts)):
        found[:, at(k)] = part

    def refine(state):
        short = system[width:, :] - wide_product(found[...], system)
        moved, size = 0.0, 0.0
        for k, part in enumerate(apply([short[:, at(k)] for k in range(count)])):
            found[:, at(k)] += part
            moved += jnp.sum(part * part)
            size += jnp.sum(found[:, at(k)] * found[:, at(k)])
        return state[0] + 1, jnp.logical_not((moved <= 1e-6 * size) & (size < 1e30))

    _, rough = lax.while_loop(lambda state: state[1] & (state[0] < 3), refine, (0, True))

    @pl.when(rough)
    def _():
        found[...] = jnp.zeros_like(found)
        gained, short, ahead = (slice(i * padded, (i + 1) * padded) for i in range(3))
        tiny = 1e-30

        def norms(there):
            return jnp.sum(work[there, :] * work[there, :], axis=1, keepdims=True)

        def restart(_, carry):
            work[short, :] = system[width:, :] - exact_product(found[...], system[:width, :])
            work[ahead, :] = work[short, :]
            work[gained, :] = jnp.zeros_like(found)
            first = norms(short)

            def advance(state):
                turn, _, size = state
                image = exact_product(work[ahead, :], system[:width, :])
                far = size / jnp.maximum(jnp.sum(work[ahead, :] * image, axis=1, keepdims=True), tiny)
                work[gained, :] += far * work[ahead, :]
                work[short, :] -= far * image
                after = norms(short)
                work[ahead, :] = work[short, :] + after / jnp.maximum(size, tiny) * work[ahead, :]
                return turn + 1, jnp.max(after - 1e-12 * first) > 0.0, after

            lax.while_loop(lambda state: state[1] & (state[0] < 500), advance, (0, True, first))
            found[...] += work[gained, :]
            return carry

        lax.fori_loop(0, 3, restart, 0)

    change = found[...]
    added = dot(change.astype(bf16), turned[...])
    updated[...] = predictions[...] + added[:classes]
    at_row = lax.broadcasted_iota(jnp.int32, (2 * tile, 2 * tile), 0)
    at_lane = lax.broadcasted_iota(jnp.int32, (2 * tile, 2 * tile), 1)
    goal = (at_row % tile) // own_width * (2 * own_width) + at_row // tile * own_width + at_row % own_width
    order = (goal == at_lane).astype(bf16)
    for u in range(width // (2 * tile)):
        one, two = slice(u * tile, (u + 1) * tile), slice(width // 2 + u * tile, width // 2 + (u + 1) * tile)
        part = jnp.concatenate([found[:, one] + old[:, one], found[:, two] + old[:, two]], axis=1)
        high, low, last = (dot(piece, order) for piece in three(part))
        moved = (high + low) + last
        coeffs[:, 2 * u * tile : 2 * (u + 1) * tile] = moved[:classes]


def solve(place, mine, other, mine_old, other_old, turned, predictions, total_rows):
    width, (classes, rows) = turned.shape[0], predictions.shape
    here = pl.BlockSpec(memory_space=pltpu.VMEM)
    padded = -(-classes // 16) * 16
    return pl.pallas_call(
        functools.partial(solve_kernel, float(total_rows)),
        out_shape=(
            jax.ShapeDtypeStruct((classes, width), f32),
            jax.ShapeDtypeStruct((classes, rows), f32),
        ),
        in_specs=[pl.BlockSpec(memory_space=pltpu.SMEM)] + [here] * 6,
        out_specs=(here, here),
        scratch_shapes=[
            pltpu.VMEM((width + padded, width), f32),
            pltpu.VMEM((width + padded, width), f32),
            pltpu.VMEM((width, step), bf16),
            pltpu.VMEM((width, step), bf16),
            pltpu.VMEM((width, width), bf16),
            pltpu.VMEM((width, width), bf16),
            pltpu.VMEM((width, width), bf16),
            pltpu.VMEM((width, width), bf16),
            pltpu.VMEM((padded, width), f32),
            pltpu.VMEM((padded, width), f32),
        ],
        compiler_params=pltpu.CompilerParams(vmem_limit_bytes=38 * 1024 * 1024),
        name="solve",
    )(place, mine, other, mine_old, other_old, turned, predictions)


def exchange(x, axes):
    return lax.all_to_all(x, axes, 0, 0, tiled=True)


def gather(x, axes):
    return exchange(jnp.broadcast_to(x[None], (lax.axis_size(axes), *x.shape)), axes)


def swap(x):
    return lax.ppermute(x, "core", [(0, 1), (1, 0)])


def local(frames, freqs, phase, labels, predictions, coeffs_old):
    rows, classes = predictions.shape
    depth, own = freqs.shape
    width = phase.shape[0]
    cores = lax.axis_size("core")
    devices = width // own
    place = lax.axis_index("core").astype(jnp.int32)[None]
    first = lax.reduce_precision(coeffs_old, 8, 7)
    second = lax.reduce_precision(coeffs_old - first, 8, 7)
    olds = [part.astype(bf16) for part in (first, second, coeffs_old - first - second)]
    filled = -(-(depth + 3 * (classes - tile)) // tile) * tile
    lanes = filled + 3 * tile

    def put(x, start):
        return jnp.pad(x, ((0, 0), (start, lanes - start - x.shape[1])))

    sent = put(freqs.T, 0)
    for i, part in enumerate(olds):
        sent += put(part[:, tile:], depth + i * (classes - tile)) + put(part[:, :tile], filled + i * tile)
    mine_sent = gather(sent, "z").reshape(-1, sent.shape[1])
    mine_sent = gather(mine_sent, ("x", "y")).reshape(width // cores, sent.shape[1])
    other_sent = swap(mine_sent)
    phase = phase.reshape(devices // cores, cores, own).swapaxes(0, 1).reshape(width, 1)
    turned, packed = moments(
        place, mine_sent, other_sent, frames.T, phase, labels[None, :], predictions.T
    )
    shares = lax.axis_size("z")
    sums = (packed[0] + swap(packed[1])).reshape(lax.axis_size(("x", "y")), -1, tile)
    sums = exchange(sums, ("x", "y")).sum(0)
    share = sums.shape[0]
    sums = jnp.pad(sums, ((0, -share % (8 * shares)), (0, 0)))
    sums = exchange(sums.reshape(shares, -1, tile), "z").sum(0)
    sums = gather(sums, "z").reshape(-1, tile)[:share]
    mine = gather(sums, ("x", "y")).reshape(-1, tile)
    other = swap(mine)
    coeffs_new, new_predictions = solve(
        place, mine, other, mine_sent, other_sent, turned, predictions.T, rows * devices
    )
    return new_predictions.T, coeffs_new.T


def solution(mesh):
    chips = mesh.devices.reshape(4, 4, 8, 2)
    inner = Mesh(chips, ("x", "y", "z", "core"))
    every = ("x", "y", "z", "core")
    placed = (P(every, None), P(None, every), P(), P(every), P(every, None), P(every, None))
    return jax.shard_map(
        local, mesh=inner, in_specs=placed, out_specs=(P(every, None), P()), check_vma=False
    )
```

```python
import functools

import jax
import jax.numpy as jnp
import numpy as np
from jax import lax
from jax.experimental import pallas as pl
from jax.experimental.pallas import tpu as pltpu
from jax.sharding import Mesh, PartitionSpec as P

f32 = jnp.float32
bf16 = jnp.bfloat16
root_two = 1.4142135623730951
ridge = 1.0
tile = 128
step = 256
own_width = 4
depth_of = 440
NN = (((1,), (0,)), ((), ()))
NT = (((1,), (1,)), ((), ()))


def cosine_coefficients(degree):
    nodes = 0.125 * np.cos(np.pi * (np.arange(400) + 0.5) / 400) + 0.125
    wanted = root_two * np.cos(2 * np.pi * np.sqrt(nodes))
    fitted = np.polynomial.chebyshev.Chebyshev.fit(nodes, wanted, degree, domain=[0, 0.25])
    return [float(c) for c in fitted.convert(kind=np.polynomial.Polynomial).coef]


cosine = cosine_coefficients(6)


def features_of(angles):
    turns = angles * (0.5 / np.pi)
    part = turns - jnp.round(turns)
    square = part * part
    value = cosine[-1] * square + cosine[-2]
    for coefficient in cosine[-3::-1]:
        value = value * square + coefficient
    return value.astype(bf16)


def dot(a, b, dims=NN):
    return lax.dot_general(a, b, dims, preferred_element_type=f32)


def split(x):
    high = x.astype(bf16)
    return high, (x - high.astype(f32)).astype(bf16)


def product(a, b):
    rows = a[0].shape[0]
    both = dot(jnp.concatenate(a, axis=0), b[0])
    return both[:rows] + (both[rows:] + dot(a[0], b[1]))


def exact_product(a, b):
    return lax.dot_general(a, b, NN, precision=lax.Precision.HIGHEST, preferred_element_type=f32)


def three(x):
    high, low = split(x)
    return high, low, (x - high.astype(f32) - low.astype(f32)).astype(bf16)


def wide_product(x, wide):
    rows, depth = x.shape
    parts = jnp.concatenate(three(x), axis=0)
    result = []
    for j in range(depth // step):
        high, low, last = three(wide[:depth, j * step : (j + 1) * step])
        one = dot(parts, high)
        two = dot(parts[: 2 * rows], low)
        small = one[2 * rows :] + two[rows:] + dot(parts[:rows], last)
        result.append(one[:rows] + ((one[rows : 2 * rows] + two[:rows]) + small))
    return jnp.concatenate(result, axis=1)


def pairs(blocks):
    return [(a, b) for a in range(blocks) for b in range(a)]


def layout(width, classes):
    blocks = width // tile
    below = len(pairs(blocks)) * tile
    lower = below + blocks // 2 * tile
    each = -(-(classes + 1) // 16) * 16
    return blocks, below, lower, each, lower + blocks * each


def coordinates(side):
    return tuple(lax.broadcasted_iota(jnp.int32, (side, side), axis) for axis in (0, 1))


def moment_kernel(
    place, mine, other, frames, phase, labels, predictions, turned, keep, send,
    packed, residual, sems,
):
    width, (classes, rows) = phase.shape[0], predictions.shape
    depth = frames.shape[0]
    blocks, below, lower, each, total = layout(width, classes)
    half = total // 2
    core = place[0]
    at_row, at_lane = coordinates(tile)
    residual[...] = jnp.zeros_like(residual)
    onehot = labels[...] == lax.broadcasted_iota(jnp.int32, (classes, rows), 0)
    residual[:classes, :] = onehot.astype(f32) - predictions[...]
    wanted = residual[...].astype(bf16)
    row = 0
    for i in range(width // step):
        here = slice(i * step, (i + 1) * step)
        first = (i * step) % (width // 2)
        side = core == (i * step) // (width // 2)
        there = slice(first, first + step)
        freqs = jnp.where(side, mine[there, :depth], other[there, :depth])
        angles = dot(freqs, frames[...]) + phase[here, :]
        block = features_of(angles)
        turned[here, :] = block
        gram = dot(block, turned[: (i + 1) * step, :], NT)
        cross = dot(wanted, block, NT)
        for j in range(step // tile):
            a = i * (step // tile) + j
            for b in range(a):
                packed[row // half, row % half : row % half + tile, :] = gram[
                    j * tile : (j + 1) * tile, b * tile : (b + 1) * tile
                ]
                row += tile
            start = lower + a * each - half
            packed[1, start : start + each, :] = cross[:, j * tile : (j + 1) * tile]
        even = gram[:tile, 2 * i * tile : (2 * i + 1) * tile]
        odd = gram[tile:, (2 * i + 1) * tile :]
        start = below + i * tile
        packed[start // half, start % half : start % half + tile, :] = jnp.where(at_row >= at_lane, even, odd)
        start = lower + (2 * i + 1) * each + classes - half
        packed[1, start : start + 1, :] = jnp.sum(jnp.where(at_row == at_lane, odd, 0.0), axis=0, keepdims=True)
    copies = [
        pltpu.make_async_copy(packed.at[core], keep, sems.at[0]),
        pltpu.make_async_copy(packed.at[1 - core], send, sems.at[1]),
    ]
    for copy in copies:
        copy.start()
    for copy in copies:
        copy.wait()


def moments(place, mine, other, frames, phase, labels, predictions):
    width, (classes, rows) = phase.shape[0], predictions.shape
    _, _, _, each, total = layout(width, classes)
    here = pl.BlockSpec(memory_space=pltpu.VMEM)
    half = jax.ShapeDtypeStruct((total // 2, tile), f32)
    return pl.pallas_call(
        moment_kernel,
        out_shape=(jax.ShapeDtypeStruct((width, rows), bf16), half, half),
        in_specs=[pl.BlockSpec(memory_space=pltpu.SMEM)] + [here] * 6,
        out_specs=(here, pl.BlockSpec(memory_space=pl.ANY), pl.BlockSpec(memory_space=pl.ANY)),
        scratch_shapes=[
            pltpu.VMEM((2, total // 2, tile), f32),
            pltpu.VMEM((each, rows), f32),
            pltpu.SemaphoreType.DMA((2,)),
        ],
        compiler_params=pltpu.CompilerParams(vmem_limit_bytes=18 * 1024 * 1024),
        name="moments",
    )(place, mine, other, frames, phase, labels, predictions)


def inverse(a, eye, bound, steps, loop=False, correct=True):
    scale = 2.0 / (2.0 * ridge + bound)

    def advance(k, state):
        x, rest, spread = state
        gain = 2.0 / (2.0 - spread * spread)
        spread = spread * spread / (2.0 - spread * spread)
        parts = split(rest)
        x = gain * (x + product(split(x), parts))
        if loop or k < steps - 1:
            rest = gain * product(parts, parts) - spread * eye
        return x, rest, spread

    state = scale * eye, eye - scale * a, bound / (2.0 * ridge + bound)
    if loop:
        state = lax.fori_loop(0, steps, advance, state[:2] + (jnp.float32(state[2]),))
    else:
        x, rest, spread = state
        gain = 2.0 / (2.0 - spread * spread)
        spread = spread * spread / (2.0 - spread * spread)
        parts = split(rest)
        state = gain * (x + scale * rest), gain * product(parts, parts) - spread * eye, spread
        for k in range(1, steps):
            state = advance(k, state)
    x = state[0]
    if not correct:
        return x
    missing = eye - product(split(a), split(x))
    return x + product(split(x), split(missing))


def solve_kernel(
    total_rows, place, mine, other, mine_old, other_old, turned, predictions, coeffs, updated,
    system, work, inv_h, inv_l, low_h, low_l, up_h, up_l, found, old,
):
    width = turned.shape[0]
    classes = predictions.shape[0]
    blocks, below, lower, each, total = layout(width, classes)
    count = width // step
    scale = 1.0 / total_rows
    padded = found.shape[0]
    core = place[0]

    def sums(start, rows):
        part, start = divmod(start, total // 2)
        there = slice(start, start + rows)
        return jnp.where(core == part, mine[there, :], other[there, :])

    def at(k):
        return slice(k * step, (k + 1) * step)

    eye = functools.reduce(jnp.equal, coordinates(step)).astype(f32)
    at_row, at_lane = coordinates(tile)
    for t, (a, b) in enumerate(pairs(blocks)):
        part = sums(t * tile, tile) * scale
        system[a * tile : (a + 1) * tile, b * tile : (b + 1) * tile] = part
        system[b * tile : (b + 1) * tile, a * tile : (a + 1) * tile] = part.T
    for i in range(blocks // 2):
        part = sums(below + i * tile, tile)
        other_way = part.T
        diagonal = sums(lower + (2 * i + 1) * each + classes, 1)
        even = jnp.where(at_row >= at_lane, part, other_way)
        odd = jnp.where(at_row == at_lane, diagonal, jnp.where(at_row < at_lane, part, other_way))
        for a, part in ((2 * i, even), (2 * i + 1, odd)):
            there = slice(a * tile, (a + 1) * tile)
            system[there, there] = part * scale + ridge * eye[:tile, :tile]
    for m in range(blocks):
        lanes = slice(m * tile, (m + 1) * tile)
        there = slice(m * tile % (width // 2), m * tile % (width // 2) + tile)
        side = core == m * tile // (width // 2)
        main, rest = 0.0, 0.0
        ends = jnp.where(side, mine_old[there, 3 * tile : 4 * tile], other_old[there, 3 * tile : 4 * tile])
        ends = ends.astype(f32).T
        first = depth_of % tile
        for i in range(3):
            lane = slice((4 + i) * tile, (5 + i) * tile)
            main = main + jnp.where(side, mine_old[there, lane], other_old[there, lane]).astype(f32)
            rest = rest + ends[first + i * (classes - tile) : first + (i + 1) * (classes - tile)]
        old[:tile, lanes] = main.T
        old[tile:, lanes] = jnp.zeros((padded - tile, tile), f32)
        old[tile:classes, lanes] = rest
        valid = lax.broadcasted_iota(jnp.int32, (padded, tile), 0) < classes
        system[width:, lanes] = jnp.where(valid, sums(lower + m * each, padded) * scale - old[:, lanes], 0.0)
    parts = []
    for k in range(count):
        source = system if k == 0 else work
        block = source[at(k), at(k)]

        def invert(bound, steps, **options):
            inv_h[at(k), :], inv_l[at(k), :] = split(inverse(block, eye, bound, steps, **options))

        if k == 0:
            invert(2.0 * step, 7)
        else:
            small = jnp.max(jnp.sum(jnp.abs(block - ridge * eye), axis=0)) <= 6.0
            pl.when(small)(functools.partial(invert, 6.0, 4, correct=False))
            pl.when(jnp.logical_not(small))(functools.partial(invert, 2.0 * step, 7, loop=True))
        x = inv_h[at(k), :], inv_l[at(k), :]
        column = product(split(source[(k + 1) * step :, at(k)]), x)
        parts.append(column[-padded:])
        if k == count - 1:
            break
        after = slice((k + 1) * step, width)
        column = split(column)
        low_h[after, at(k)], low_l[after, at(k)] = column[0][:-padded], column[1][:-padded]
        row = split(source[at(k), after])
        up_h[at(k), after], up_l[at(k), after] = row
        work[(k + 1) * step :, after] = source[(k + 1) * step :, after] - product(column, row)

    def backward(parts):
        for k in reversed(range(1, count)):
            before = slice(0, k * step)
            less = product(split(parts[k]), (low_h[at(k), before], low_l[at(k), before]))
            for i in range(k):
                parts[i] = parts[i] - less[:, i * step : (i + 1) * step]
        return parts

    def apply(parts):
        for k in range(count):
            now = parts[k] = product(split(parts[k]), (inv_h[at(k), :], inv_l[at(k), :]))
            if k < count - 1:
                after = slice((k + 1) * step, width)
                less = product(split(now), (up_h[at(k), after], up_l[at(k), after]))
                for i in range(k + 1, count):
                    parts[i] = parts[i] - less[:, (i - k - 1) * step : (i - k) * step]
        return backward(parts)

    for k, part in enumerate(backward(parts)):
        found[:, at(k)] = part

    def refine(state):
        short = system[width:, :] - wide_product(found[...], system)
        moved, size = 0.0, 0.0
        for k, part in enumerate(apply([short[:, at(k)] for k in range(count)])):
            found[:, at(k)] += part
            moved += jnp.sum(part * part)
            size += jnp.sum(found[:, at(k)] * found[:, at(k)])
        return state[0] + 1, jnp.logical_not((moved <= 1e-6 * size) & (size < 1e30))

    _, rough = lax.while_loop(lambda state: state[1] & (state[0] < 3), refine, (0, True))

    @pl.when(rough)
    def _():
        found[...] = jnp.zeros_like(found)
        gained, short, ahead = (slice(i * padded, (i + 1) * padded) for i in range(3))
        tiny = 1e-30

        def norms(there):
            return jnp.sum(work[there, :] * work[there, :], axis=1, keepdims=True)

        def restart(_, carry):
            work[short, :] = system[width:, :] - exact_product(found[...], system[:width, :])
            work[ahead, :] = work[short, :]
            work[gained, :] = jnp.zeros_like(found)
            first = norms(short)

            def advance(state):
                turn, _, size = state
                image = exact_product(work[ahead, :], system[:width, :])
                far = size / jnp.maximum(jnp.sum(work[ahead, :] * image, axis=1, keepdims=True), tiny)
                work[gained, :] += far * work[ahead, :]
                work[short, :] -= far * image
                after = norms(short)
                work[ahead, :] = work[short, :] + after / jnp.maximum(size, tiny) * work[ahead, :]
                return turn + 1, jnp.max(after - 1e-12 * first) > 0.0, after

            lax.while_loop(lambda state: state[1] & (state[0] < 500), advance, (0, True, first))
            found[...] += work[gained, :]
            return carry

        lax.fori_loop(0, 3, restart, 0)

    change = found[...]
    added = dot(change.astype(bf16), turned[...])
    updated[...] = predictions[...] + added[:classes]
    at_row = lax.broadcasted_iota(jnp.int32, (2 * tile, 2 * tile), 0)
    at_lane = lax.broadcasted_iota(jnp.int32, (2 * tile, 2 * tile), 1)
    goal = (at_row % tile) // own_width * (2 * own_width) + at_row // tile * own_width + at_row % own_width
    order = (goal == at_lane).astype(bf16)
    for u in range(width // (2 * tile)):
        one, two = slice(u * tile, (u + 1) * tile), slice(width // 2 + u * tile, width // 2 + (u + 1) * tile)
        part = jnp.concatenate([found[:, one] + old[:, one], found[:, two] + old[:, two]], axis=1)
        high, low, last = (dot(piece, order) for piece in three(part))
        moved = (high + low) + last
        coeffs[:, 2 * u * tile : 2 * (u + 1) * tile] = moved[:classes]


def solve(place, mine, other, mine_old, other_old, turned, predictions, total_rows):
    width, (classes, rows) = turned.shape[0], predictions.shape
    here = pl.BlockSpec(memory_space=pltpu.VMEM)
    padded = -(-classes // 16) * 16
    return pl.pallas_call(
        functools.partial(solve_kernel, float(total_rows)),
        out_shape=(
            jax.ShapeDtypeStruct((classes, width), f32),
            jax.ShapeDtypeStruct((classes, rows), f32),
        ),
        in_specs=[pl.BlockSpec(memory_space=pltpu.SMEM)] + [here] * 6,
        out_specs=(here, here),
        scratch_shapes=[
            pltpu.VMEM((width + padded, width), f32),
            pltpu.VMEM((width + padded, width), f32),
            pltpu.VMEM((width, step), bf16),
            pltpu.VMEM((width, step), bf16),
            pltpu.VMEM((width, width), bf16),
            pltpu.VMEM((width, width), bf16),
            pltpu.VMEM((width, width), bf16),
            pltpu.VMEM((width, width), bf16),
            pltpu.VMEM((padded, width), f32),
            pltpu.VMEM((padded, width), f32),
        ],
        compiler_params=pltpu.CompilerParams(vmem_limit_bytes=38 * 1024 * 1024),
        name="solve",
    )(place, mine, other, mine_old, other_old, turned, predictions)


def exchange(x, axes):
    return lax.all_to_all(x, axes, 0, 0, tiled=True)


def gather(x, axes):
    return exchange(jnp.broadcast_to(x[None], (lax.axis_size(axes), *x.shape)), axes)


def swap(x):
    return lax.ppermute(x, "core", [(0, 1), (1, 0)])


def local(frames, freqs, phase, labels, predictions, coeffs_old):
    rows, classes = predictions.shape
    depth, own = freqs.shape
    width = phase.shape[0]
    cores = lax.axis_size("core")
    devices = width // own
    place = lax.axis_index("core").astype(jnp.int32)[None]
    first = lax.reduce_precision(coeffs_old, 8, 7)
    second = lax.reduce_precision(coeffs_old - first, 8, 7)
    olds = [part.astype(bf16) for part in (first, second, coeffs_old - first - second)]
    filled = -(-(depth + 3 * (classes - tile)) // tile) * tile
    lanes = filled + 3 * tile

    def put(x, start):
        return jnp.pad(x, ((0, 0), (start, lanes - start - x.shape[1])))

    sent = put(freqs.T, 0)
    for i, part in enumerate(olds):
        sent += put(part[:, tile:], depth + i * (classes - tile)) + put(part[:, :tile], filled + i * tile)
    mine_sent = gather(sent, "z").reshape(-1, sent.shape[1])
    mine_sent = gather(mine_sent, ("x", "y")).reshape(width // cores, sent.shape[1])
    other_sent = swap(mine_sent)
    phase = phase.reshape(devices // cores, cores, own).swapaxes(0, 1).reshape(width, 1)
    turned, keep, send = moments(
        place, mine_sent, other_sent, frames.T, phase, labels[None, :], predictions.T
    )
    shares = lax.axis_size("z")
    sums = (keep + swap(send)).reshape(lax.axis_size(("x", "y")), -1, tile)
    sums = exchange(sums, ("x", "y")).sum(0)
    share = sums.shape[0]
    sums = jnp.pad(sums, ((0, -share % (8 * shares)), (0, 0)))
    sums = exchange(sums.reshape(shares, -1, tile), "z").sum(0)
    sums = gather(sums, "z").reshape(-1, tile)[:share]
    mine = gather(sums, ("x", "y")).reshape(-1, tile)
    other = swap(mine)
    coeffs_new, new_predictions = solve(
        place, mine, other, mine_sent, other_sent, turned, predictions.T, rows * devices
    )
    return new_predictions.T, coeffs_new.T


def solution(mesh):
    chips = mesh.devices.reshape(4, 4, 8, 2)
    inner = Mesh(chips, ("x", "y", "z", "core"))
    every = ("x", "y", "z", "core")
    placed = (P(every, None), P(None, every), P(), P(every), P(every, None), P(every, None))
    return jax.shard_map(
        local, mesh=inner, in_specs=placed, out_specs=(P(every, None), P()), check_vma=False
    )
```

```python
import functools

import jax
import jax.numpy as jnp
import numpy as np
from jax import lax
from jax.experimental import pallas as pl
from jax.experimental.pallas import tpu as pltpu
from jax.sharding import Mesh, PartitionSpec as P

f32 = jnp.float32
bf16 = jnp.bfloat16
root_two = 1.4142135623730951
ridge = 1.0
tile = 128
step = 256
own_width = 4
depth_of = 440
NN = (((1,), (0,)), ((), ()))
NT = (((1,), (1,)), ((), ()))


def cosine_coefficients(degree):
    nodes = 0.125 * np.cos(np.pi * (np.arange(400) + 0.5) / 400) + 0.125
    wanted = root_two * np.cos(2 * np.pi * np.sqrt(nodes))
    fitted = np.polynomial.chebyshev.Chebyshev.fit(nodes, wanted, degree, domain=[0, 0.25])
    return [float(c) for c in fitted.convert(kind=np.polynomial.Polynomial).coef]


cosine = cosine_coefficients(6)


def features_of(angles):
    turns = angles * (0.5 / np.pi)
    part = turns - jnp.round(turns)
    square = part * part
    value = cosine[-1] * square + cosine[-2]
    for coefficient in cosine[-3::-1]:
        value = value * square + coefficient
    return value.astype(bf16)


def dot(a, b, dims=NN):
    return lax.dot_general(a, b, dims, preferred_element_type=f32)


def split(x):
    high = x.astype(bf16)
    return high, (x - high.astype(f32)).astype(bf16)


def product(a, b):
    rows = a[0].shape[0]
    both = dot(jnp.concatenate(a, axis=0), b[0])
    return both[:rows] + (both[rows:] + dot(a[0], b[1]))


def exact_product(a, b):
    return lax.dot_general(a, b, NN, precision=lax.Precision.HIGHEST, preferred_element_type=f32)


def three(x):
    high, low = split(x)
    return high, low, (x - high.astype(f32) - low.astype(f32)).astype(bf16)


def wide_product(x, wide):
    rows, depth = x.shape
    parts = jnp.concatenate(three(x), axis=0)
    result = []
    for j in range(depth // step):
        high, low, last = three(wide[:depth, j * step : (j + 1) * step])
        one = dot(parts, high)
        two = dot(parts[: 2 * rows], low)
        small = one[2 * rows :] + two[rows:] + dot(parts[:rows], last)
        result.append(one[:rows] + ((one[rows : 2 * rows] + two[:rows]) + small))
    return jnp.concatenate(result, axis=1)


def pairs(blocks):
    return [(a, b) for a in range(blocks) for b in range(a)]


def layout(width, classes):
    blocks = width // tile
    below = len(pairs(blocks)) * tile
    lower = below + blocks // 2 * tile
    each = -(-(classes + 1) // 16) * 16
    return blocks, below, lower, each, lower + blocks * each


def coordinates(side):
    return tuple(lax.broadcasted_iota(jnp.int32, (side, side), axis) for axis in (0, 1))


def moment_kernel(
    place, mine, other, frames, labels, predictions, turned, keep, send,
    packed, residual, sems,
):
    width, (classes, rows) = turned.shape[0], predictions.shape
    depth = frames.shape[0]
    spare = classes + 1 - tile
    blocks, below, lower, each, total = layout(width, classes)
    half = total // 2
    core = place[0]
    at_row, at_lane = coordinates(tile)
    residual[...] = jnp.zeros_like(residual)
    onehot = labels[...] == lax.broadcasted_iota(jnp.int32, (classes, rows), 0)
    residual[:classes, :] = onehot.astype(f32) - predictions[...]
    wanted = residual[...].astype(bf16)
    row = 0
    for i in range(width // step):
        here = slice(i * step, (i + 1) * step)
        first = (i * step) % (width // 2)
        side = core == (i * step) // (width // 2)
        there = slice(first, first + step)
        freqs = jnp.where(side, mine[there, : 4 * tile], other[there, : 4 * tile])
        phase = 0.0
        for n in range(1, 4):
            phase = phase + freqs[:, depth + n * spare - 1 : depth + n * spare].astype(f32)
        angles = dot(freqs[:, :depth], frames[...]) + phase
        block = features_of(angles)
        turned[here, :] = block
        gram = dot(block, turned[: (i + 1) * step, :], NT)
        cross = dot(wanted, block, NT)
        for j in range(step // tile):
            a = i * (step // tile) + j
            for b in range(a):
                packed[row // half, row % half : row % half + tile, :] = gram[
                    j * tile : (j + 1) * tile, b * tile : (b + 1) * tile
                ]
                row += tile
            start = lower + a * each - half
            packed[1, start : start + each, :] = cross[:, j * tile : (j + 1) * tile]
        even = gram[:tile, 2 * i * tile : (2 * i + 1) * tile]
        odd = gram[tile:, (2 * i + 1) * tile :]
        start = below + i * tile
        packed[start // half, start % half : start % half + tile, :] = jnp.where(at_row >= at_lane, even, odd)
        start = lower + (2 * i + 1) * each + classes - half
        packed[1, start : start + 1, :] = jnp.sum(jnp.where(at_row == at_lane, odd, 0.0), axis=0, keepdims=True)
    copies = [
        pltpu.make_async_copy(packed.at[core], keep, sems.at[0]),
        pltpu.make_async_copy(packed.at[1 - core], send, sems.at[1]),
    ]
    for copy in copies:
        copy.start()
    for copy in copies:
        copy.wait()


def moments(place, mine, other, frames, labels, predictions):
    width, (classes, rows) = 2 * mine.shape[0], predictions.shape
    _, _, _, each, total = layout(width, classes)
    here = pl.BlockSpec(memory_space=pltpu.VMEM)
    half = jax.ShapeDtypeStruct((total // 2, tile), f32)
    return pl.pallas_call(
        moment_kernel,
        out_shape=(jax.ShapeDtypeStruct((width, rows), bf16), half, half),
        in_specs=[pl.BlockSpec(memory_space=pltpu.SMEM)] + [here] * 5,
        out_specs=(here, pl.BlockSpec(memory_space=pl.ANY), pl.BlockSpec(memory_space=pl.ANY)),
        scratch_shapes=[
            pltpu.VMEM((2, total // 2, tile), f32),
            pltpu.VMEM((each, rows), f32),
            pltpu.SemaphoreType.DMA((2,)),
        ],
        compiler_params=pltpu.CompilerParams(vmem_limit_bytes=18 * 1024 * 1024),
        name="moments",
    )(place, mine, other, frames, labels, predictions)


def inverse(a, eye, bound, steps, loop=False, correct=True):
    scale = 2.0 / (2.0 * ridge + bound)

    def advance(k, state):
        x, rest, spread = state
        gain = 2.0 / (2.0 - spread * spread)
        spread = spread * spread / (2.0 - spread * spread)
        parts = split(rest)
        x = gain * (x + product(split(x), parts))
        if loop or k < steps - 1:
            rest = gain * product(parts, parts) - spread * eye
        return x, rest, spread

    state = scale * eye, eye - scale * a, bound / (2.0 * ridge + bound)
    if loop:
        state = lax.fori_loop(0, steps, advance, state[:2] + (jnp.float32(state[2]),))
    else:
        x, rest, spread = state
        gain = 2.0 / (2.0 - spread * spread)
        spread = spread * spread / (2.0 - spread * spread)
        parts = split(rest)
        state = gain * (x + scale * rest), gain * product(parts, parts) - spread * eye, spread
        for k in range(1, steps):
            state = advance(k, state)
    x = state[0]
    if not correct:
        return x
    missing = eye - product(split(a), split(x))
    return x + product(split(x), split(missing))


def solve_kernel(
    total_rows, place, mine, other, mine_old, other_old, turned, predictions, coeffs, updated,
    system, work, inv_h, inv_l, low_h, low_l, up_h, up_l, found, old,
):
    width = turned.shape[0]
    classes = predictions.shape[0]
    blocks, below, lower, each, total = layout(width, classes)
    count = width // step
    scale = 1.0 / total_rows
    padded = found.shape[0]
    core = place[0]

    def sums(start, rows):
        part, start = divmod(start, total // 2)
        there = slice(start, start + rows)
        return jnp.where(core == part, mine[there, :], other[there, :])

    def at(k):
        return slice(k * step, (k + 1) * step)

    eye = functools.reduce(jnp.equal, coordinates(step)).astype(f32)
    at_row, at_lane = coordinates(tile)
    for t, (a, b) in enumerate(pairs(blocks)):
        part = sums(t * tile, tile) * scale
        system[a * tile : (a + 1) * tile, b * tile : (b + 1) * tile] = part
        system[b * tile : (b + 1) * tile, a * tile : (a + 1) * tile] = part.T
    for i in range(blocks // 2):
        part = sums(below + i * tile, tile)
        other_way = part.T
        diagonal = sums(lower + (2 * i + 1) * each + classes, 1)
        even = jnp.where(at_row >= at_lane, part, other_way)
        odd = jnp.where(at_row == at_lane, diagonal, jnp.where(at_row < at_lane, part, other_way))
        for a, part in ((2 * i, even), (2 * i + 1, odd)):
            there = slice(a * tile, (a + 1) * tile)
            system[there, there] = part * scale + ridge * eye[:tile, :tile]
    for m in range(blocks):
        lanes = slice(m * tile, (m + 1) * tile)
        there = slice(m * tile % (width // 2), m * tile % (width // 2) + tile)
        side = core == m * tile // (width // 2)
        main, rest = 0.0, 0.0
        ends = jnp.where(side, mine_old[there, 3 * tile : 4 * tile], other_old[there, 3 * tile : 4 * tile])
        ends = ends.astype(f32).T
        first, spare = depth_of % tile, classes + 1 - tile
        for i in range(3):
            lane = slice((4 + i) * tile, (5 + i) * tile)
            main = main + jnp.where(side, mine_old[there, lane], other_old[there, lane]).astype(f32)
            rest = rest + ends[first + i * spare : first + i * spare + classes - tile]
        old[:tile, lanes] = main.T
        old[tile:, lanes] = jnp.zeros((padded - tile, tile), f32)
        old[tile:classes, lanes] = rest
        valid = lax.broadcasted_iota(jnp.int32, (padded, tile), 0) < classes
        system[width:, lanes] = jnp.where(valid, sums(lower + m * each, padded) * scale - old[:, lanes], 0.0)
    parts = []
    for k in range(count):
        source = system if k == 0 else work
        block = source[at(k), at(k)]

        def invert(bound, steps, **options):
            inv_h[at(k), :], inv_l[at(k), :] = split(inverse(block, eye, bound, steps, **options))

        if k == 0:
            invert(2.0 * step, 7)
        else:
            small = jnp.max(jnp.sum(jnp.abs(block - ridge * eye), axis=0)) <= 6.0
            pl.when(small)(functools.partial(invert, 6.0, 4, correct=False))
            pl.when(jnp.logical_not(small))(functools.partial(invert, 2.0 * step, 7, loop=True))
        x = inv_h[at(k), :], inv_l[at(k), :]
        column = product(split(source[(k + 1) * step :, at(k)]), x)
        parts.append(column[-padded:])
        if k == count - 1:
            break
        after = slice((k + 1) * step, width)
        column = split(column)
        low_h[after, at(k)], low_l[after, at(k)] = column[0][:-padded], column[1][:-padded]
        row = split(source[at(k), after])
        up_h[at(k), after], up_l[at(k), after] = row
        work[(k + 1) * step :, after] = source[(k + 1) * step :, after] - product(column, row)

    def backward(parts):
        for k in reversed(range(1, count)):
            before = slice(0, k * step)
            less = product(split(parts[k]), (low_h[at(k), before], low_l[at(k), before]))
            for i in range(k):
                parts[i] = parts[i] - less[:, i * step : (i + 1) * step]
        return parts

    def apply(parts):
        for k in range(count):
            now = parts[k] = product(split(parts[k]), (inv_h[at(k), :], inv_l[at(k), :]))
            if k < count - 1:
                after = slice((k + 1) * step, width)
                less = product(split(now), (up_h[at(k), after], up_l[at(k), after]))
                for i in range(k + 1, count):
                    parts[i] = parts[i] - less[:, (i - k - 1) * step : (i - k) * step]
        return backward(parts)

    for k, part in enumerate(backward(parts)):
        found[:, at(k)] = part

    def refine(state):
        short = system[width:, :] - wide_product(found[...], system)
        moved, size = 0.0, 0.0
        for k, part in enumerate(apply([short[:, at(k)] for k in range(count)])):
            found[:, at(k)] += part
            moved += jnp.sum(part * part)
            size += jnp.sum(found[:, at(k)] * found[:, at(k)])
        return state[0] + 1, jnp.logical_not((moved <= 1e-6 * size) & (size < 1e30))

    _, rough = lax.while_loop(lambda state: state[1] & (state[0] < 3), refine, (0, True))

    @pl.when(rough)
    def _():
        found[...] = jnp.zeros_like(found)
        gained, short, ahead = (slice(i * padded, (i + 1) * padded) for i in range(3))
        tiny = 1e-30

        def norms(there):
            return jnp.sum(work[there, :] * work[there, :], axis=1, keepdims=True)

        def restart(_, carry):
            work[short, :] = system[width:, :] - exact_product(found[...], system[:width, :])
            work[ahead, :] = work[short, :]
            work[gained, :] = jnp.zeros_like(found)
            first = norms(short)

            def advance(state):
                turn, _, size = state
                image = exact_product(work[ahead, :], system[:width, :])
                far = size / jnp.maximum(jnp.sum(work[ahead, :] * image, axis=1, keepdims=True), tiny)
                work[gained, :] += far * work[ahead, :]
                work[short, :] -= far * image
                after = norms(short)
                work[ahead, :] = work[short, :] + after / jnp.maximum(size, tiny) * work[ahead, :]
                return turn + 1, jnp.max(after - 1e-12 * first) > 0.0, after

            lax.while_loop(lambda state: state[1] & (state[0] < 500), advance, (0, True, first))
            found[...] += work[gained, :]
            return carry

        lax.fori_loop(0, 3, restart, 0)

    change = found[...]
    added = dot(change.astype(bf16), turned[...])
    updated[...] = predictions[...] + added[:classes]
    at_row = lax.broadcasted_iota(jnp.int32, (2 * tile, 2 * tile), 0)
    at_lane = lax.broadcasted_iota(jnp.int32, (2 * tile, 2 * tile), 1)
    goal = (at_row % tile) // own_width * (2 * own_width) + at_row // tile * own_width + at_row % own_width
    order = (goal == at_lane).astype(bf16)
    for u in range(width // (2 * tile)):
        one, two = slice(u * tile, (u + 1) * tile), slice(width // 2 + u * tile, width // 2 + (u + 1) * tile)
        part = jnp.concatenate([found[:, one] + old[:, one], found[:, two] + old[:, two]], axis=1)
        high, low, last = (dot(piece, order) for piece in three(part))
        moved = (high + low) + last
        coeffs[:, 2 * u * tile : 2 * (u + 1) * tile] = moved[:classes]


def solve(place, mine, other, mine_old, other_old, turned, predictions, total_rows):
    width, (classes, rows) = turned.shape[0], predictions.shape
    here = pl.BlockSpec(memory_space=pltpu.VMEM)
    padded = -(-classes // 16) * 16
    return pl.pallas_call(
        functools.partial(solve_kernel, float(total_rows)),
        out_shape=(
            jax.ShapeDtypeStruct((classes, width), f32),
            jax.ShapeDtypeStruct((classes, rows), f32),
        ),
        in_specs=[pl.BlockSpec(memory_space=pltpu.SMEM)] + [here] * 6,
        out_specs=(here, here),
        scratch_shapes=[
            pltpu.VMEM((width + padded, width), f32),
            pltpu.VMEM((width + padded, width), f32),
            pltpu.VMEM((width, step), bf16),
            pltpu.VMEM((width, step), bf16),
            pltpu.VMEM((width, width), bf16),
            pltpu.VMEM((width, width), bf16),
            pltpu.VMEM((width, width), bf16),
            pltpu.VMEM((width, width), bf16),
            pltpu.VMEM((padded, width), f32),
            pltpu.VMEM((padded, width), f32),
        ],
        compiler_params=pltpu.CompilerParams(vmem_limit_bytes=38 * 1024 * 1024),
        name="solve",
    )(place, mine, other, mine_old, other_old, turned, predictions)


def exchange(x, axes):
    return lax.all_to_all(x, axes, 0, 0, tiled=True)


def gather(x, axes):
    return exchange(jnp.broadcast_to(x[None], (lax.axis_size(axes), *x.shape)), axes)


def swap(x):
    return lax.ppermute(x, "core", [(0, 1), (1, 0)])


def local(frames, freqs, phase, labels, predictions, coeffs_old):
    rows, classes = predictions.shape
    depth, own = freqs.shape
    width = phase.shape[0]
    cores = lax.axis_size("core")
    devices = width // own
    place = lax.axis_index("core").astype(jnp.int32)[None]
    device = lax.axis_index(("x", "y", "z", "core"))
    phase = lax.dynamic_slice_in_dim(phase, device * own, own)
    held = jnp.concatenate([coeffs_old, phase[:, None]], axis=1)
    spare = classes + 1 - tile
    first = lax.reduce_precision(held, 8, 7)
    second = lax.reduce_precision(held - first, 8, 7)
    olds = [part.astype(bf16) for part in (first, second, held - first - second)]
    filled = -(-(depth + 3 * spare) // tile) * tile
    lanes = filled + 3 * tile

    def put(x, start):
        return jnp.pad(x, ((0, 0), (start, lanes - start - x.shape[1])))

    sent = put(freqs.T, 0)
    for i, part in enumerate(olds):
        sent += put(part[:, tile:], depth + i * spare) + put(part[:, :tile], filled + i * tile)
    mine_sent = gather(sent, "z").reshape(-1, sent.shape[1])
    mine_sent = gather(mine_sent, ("x", "y")).reshape(width // cores, sent.shape[1])
    other_sent = swap(mine_sent)
    turned, keep, send = moments(
        place, mine_sent, other_sent, frames.T, labels[None, :], predictions.T
    )
    shares = lax.axis_size("z")
    sums = (keep + swap(send)).reshape(lax.axis_size(("x", "y")), -1, tile)
    sums = exchange(sums, ("x", "y")).sum(0)
    share = sums.shape[0]
    sums = jnp.pad(sums, ((0, -share % (8 * shares)), (0, 0)))
    sums = exchange(sums.reshape(shares, -1, tile), "z").sum(0)
    sums = gather(sums, "z").reshape(-1, tile)[:share]
    mine = gather(sums, ("x", "y")).reshape(-1, tile)
    other = swap(mine)
    coeffs_new, new_predictions = solve(
        place, mine, other, mine_sent, other_sent, turned, predictions.T, rows * devices
    )
    return new_predictions.T, coeffs_new.T


def solution(mesh):
    chips = mesh.devices.reshape(4, 4, 8, 2)
    inner = Mesh(chips, ("x", "y", "z", "core"))
    every = ("x", "y", "z", "core")
    placed = (P(every, None), P(None, every), P(), P(every), P(every, None), P(every, None))
    return jax.shard_map(
        local, mesh=inner, in_specs=placed, out_specs=(P(every, None), P()), check_vma=False
    )
```

```python
import functools

import jax
import jax.numpy as jnp
import numpy as np
from jax import lax
from jax.experimental import pallas as pl
from jax.experimental.pallas import tpu as pltpu
from jax.sharding import Mesh, PartitionSpec as P

f32 = jnp.float32
bf16 = jnp.bfloat16
root_two = 1.4142135623730951
ridge = 1.0
tile = 128
step = 256
own_width = 4
depth_of = 440
NN = (((1,), (0,)), ((), ()))
NT = (((1,), (1,)), ((), ()))


def cosine_coefficients(degree):
    nodes = 0.125 * np.cos(np.pi * (np.arange(400) + 0.5) / 400) + 0.125
    wanted = root_two * np.cos(2 * np.pi * np.sqrt(nodes))
    fitted = np.polynomial.chebyshev.Chebyshev.fit(nodes, wanted, degree, domain=[0, 0.25])
    return [float(c) for c in fitted.convert(kind=np.polynomial.Polynomial).coef]


cosine = cosine_coefficients(6)


def features_of(angles):
    turns = angles * (0.5 / np.pi)
    part = turns - jnp.round(turns)
    square = part * part
    value = cosine[-1] * square + cosine[-2]
    for coefficient in cosine[-3::-1]:
        value = value * square + coefficient
    return value.astype(bf16)


def dot(a, b, dims=NN):
    return lax.dot_general(a, b, dims, preferred_element_type=f32)


def split(x):
    high = x.astype(bf16)
    return high, (x - high.astype(f32)).astype(bf16)


def product(a, b):
    rows = a[0].shape[0]
    both = dot(jnp.concatenate(a, axis=0), b[0])
    return both[:rows] + (both[rows:] + dot(a[0], b[1]))


def exact_product(a, b):
    return lax.dot_general(a, b, NN, precision=lax.Precision.HIGHEST, preferred_element_type=f32)


def three(x):
    high, low = split(x)
    return high, low, (x - high.astype(f32) - low.astype(f32)).astype(bf16)


def wide_product(x, wide):
    rows, depth = x.shape
    parts = jnp.concatenate(three(x), axis=0)
    result = []
    for j in range(depth // step):
        high, low, last = three(wide[:depth, j * step : (j + 1) * step])
        one = dot(parts, high)
        two = dot(parts[: 2 * rows], low)
        small = one[2 * rows :] + two[rows:] + dot(parts[:rows], last)
        result.append(one[:rows] + ((one[rows : 2 * rows] + two[:rows]) + small))
    return jnp.concatenate(result, axis=1)


def pairs(blocks):
    return [(a, b) for a in range(blocks) for b in range(a)]


def layout(width, classes):
    blocks = width // tile
    below = len(pairs(blocks)) * tile
    lower = below + blocks // 2 * tile
    each = -(-(classes + 1) // 16) * 16
    return blocks, below, lower, each, lower + blocks * each


def coordinates(side):
    return tuple(lax.broadcasted_iota(jnp.int32, (side, side), axis) for axis in (0, 1))


def moment_kernel(
    place, mine, other, frames, phase, labels, predictions, turned, keep, send,
    packed, residual, sems,
):
    width, (classes, rows) = turned.shape[0], predictions.shape
    depth = frames.shape[0]
    blocks, below, lower, each, total = layout(width, classes)
    half = total // 2
    core = place[0]
    at_row, at_lane = coordinates(tile)
    residual[...] = jnp.zeros_like(residual)
    onehot = labels[...] == lax.broadcasted_iota(jnp.int32, (classes, rows), 0)
    residual[:classes, :] = onehot.astype(f32) - predictions[...]
    wanted = residual[...].astype(bf16)
    row = 0
    for i in range(width // step):
        here = slice(i * step, (i + 1) * step)
        first = (i * step) % (width // 2)
        side = core == (i * step) // (width // 2)
        there = slice(first, first + step)
        freqs = jnp.where(side, mine[there, :depth], other[there, :depth])
        item = lax.broadcasted_iota(jnp.int32, (step, 2 * step), 0)
        goal = item // own_width * (2 * own_width) + i * step // (width // 2) * own_width + item % own_width
        chosen = goal == lax.broadcasted_iota(jnp.int32, (step, 2 * step), 1)
        shift = jnp.sum(jnp.where(chosen, phase[:, 2 * first : 2 * (first + step)], 0.0), axis=1, keepdims=True)
        angles = dot(freqs, frames[...]) + shift
        block = features_of(angles)
        turned[here, :] = block
        gram = dot(block, turned[: (i + 1) * step, :], NT)
        cross = dot(wanted, block, NT)
        for j in range(step // tile):
            a = i * (step // tile) + j
            for b in range(a):
                packed[row // half, row % half : row % half + tile, :] = gram[
                    j * tile : (j + 1) * tile, b * tile : (b + 1) * tile
                ]
                row += tile
            start = lower + a * each - half
            packed[1, start : start + each, :] = cross[:, j * tile : (j + 1) * tile]
        even = gram[:tile, 2 * i * tile : (2 * i + 1) * tile]
        odd = gram[tile:, (2 * i + 1) * tile :]
        start = below + i * tile
        packed[start // half, start % half : start % half + tile, :] = jnp.where(at_row >= at_lane, even, odd)
        start = lower + (2 * i + 1) * each + classes - half
        packed[1, start : start + 1, :] = jnp.sum(jnp.where(at_row == at_lane, odd, 0.0), axis=0, keepdims=True)
    copies = [
        pltpu.make_async_copy(packed.at[core], keep, sems.at[0]),
        pltpu.make_async_copy(packed.at[1 - core], send, sems.at[1]),
    ]
    for copy in copies:
        copy.start()
    for copy in copies:
        copy.wait()


def moments(place, mine, other, frames, phase, labels, predictions):
    width, (classes, rows) = phase.shape[1], predictions.shape
    _, _, _, each, total = layout(width, classes)
    here = pl.BlockSpec(memory_space=pltpu.VMEM)
    half = jax.ShapeDtypeStruct((total // 2, tile), f32)
    return pl.pallas_call(
        moment_kernel,
        out_shape=(jax.ShapeDtypeStruct((width, rows), bf16), half, half),
        in_specs=[pl.BlockSpec(memory_space=pltpu.SMEM)] + [here] * 6,
        out_specs=(here, pl.BlockSpec(memory_space=pl.ANY), pl.BlockSpec(memory_space=pl.ANY)),
        scratch_shapes=[
            pltpu.VMEM((2, total // 2, tile), f32),
            pltpu.VMEM((each, rows), f32),
            pltpu.SemaphoreType.DMA((2,)),
        ],
        compiler_params=pltpu.CompilerParams(vmem_limit_bytes=18 * 1024 * 1024),
        name="moments",
    )(place, mine, other, frames, phase, labels, predictions)


def inverse(a, eye, bound, steps, loop=False, correct=True):
    scale = 2.0 / (2.0 * ridge + bound)

    def advance(k, state):
        x, rest, spread = state
        gain = 2.0 / (2.0 - spread * spread)
        spread = spread * spread / (2.0 - spread * spread)
        parts = split(rest)
        x = gain * (x + product(split(x), parts))
        if loop or k < steps - 1:
            rest = gain * product(parts, parts) - spread * eye
        return x, rest, spread

    state = scale * eye, eye - scale * a, bound / (2.0 * ridge + bound)
    if loop:
        state = lax.fori_loop(0, steps, advance, state[:2] + (jnp.float32(state[2]),))
    else:
        x, rest, spread = state
        gain = 2.0 / (2.0 - spread * spread)
        spread = spread * spread / (2.0 - spread * spread)
        parts = split(rest)
        state = gain * (x + scale * rest), gain * product(parts, parts) - spread * eye, spread
        for k in range(1, steps):
            state = advance(k, state)
    x = state[0]
    if not correct:
        return x
    missing = eye - product(split(a), split(x))
    return x + product(split(x), split(missing))


def solve_kernel(
    total_rows, place, mine, other, mine_old, other_old, turned, predictions, coeffs, updated,
    system, work, inv_h, inv_l, low_h, low_l, up_h, up_l, found, old,
):
    width = turned.shape[0]
    classes = predictions.shape[0]
    blocks, below, lower, each, total = layout(width, classes)
    count = width // step
    scale = 1.0 / total_rows
    padded = found.shape[0]
    core = place[0]

    def sums(start, rows):
        part, start = divmod(start, total // 2)
        there = slice(start, start + rows)
        return jnp.where(core == part, mine[there, :], other[there, :])

    def at(k):
        return slice(k * step, (k + 1) * step)

    eye = functools.reduce(jnp.equal, coordinates(step)).astype(f32)
    at_row, at_lane = coordinates(tile)
    for t, (a, b) in enumerate(pairs(blocks)):
        part = sums(t * tile, tile) * scale
        system[a * tile : (a + 1) * tile, b * tile : (b + 1) * tile] = part
        system[b * tile : (b + 1) * tile, a * tile : (a + 1) * tile] = part.T
    for i in range(blocks // 2):
        part = sums(below + i * tile, tile)
        other_way = part.T
        diagonal = sums(lower + (2 * i + 1) * each + classes, 1)
        even = jnp.where(at_row >= at_lane, part, other_way)
        odd = jnp.where(at_row == at_lane, diagonal, jnp.where(at_row < at_lane, part, other_way))
        for a, part in ((2 * i, even), (2 * i + 1, odd)):
            there = slice(a * tile, (a + 1) * tile)
            system[there, there] = part * scale + ridge * eye[:tile, :tile]
    for m in range(blocks):
        lanes = slice(m * tile, (m + 1) * tile)
        there = slice(m * tile % (width // 2), m * tile % (width // 2) + tile)
        side = core == m * tile // (width // 2)
        main, rest = 0.0, 0.0
        ends = jnp.where(side, mine_old[there, 3 * tile : 4 * tile], other_old[there, 3 * tile : 4 * tile])
        ends = ends.astype(f32).T
        first = depth_of % tile
        for i in range(3):
            lane = slice((4 + i) * tile, (5 + i) * tile)
            main = main + jnp.where(side, mine_old[there, lane], other_old[there, lane]).astype(f32)
            rest = rest + ends[first + i * (classes - tile) : first + (i + 1) * (classes - tile)]
        old[:tile, lanes] = main.T
        old[tile:, lanes] = jnp.zeros((padded - tile, tile), f32)
        old[tile:classes, lanes] = rest
        valid = lax.broadcasted_iota(jnp.int32, (padded, tile), 0) < classes
        system[width:, lanes] = jnp.where(valid, sums(lower + m * each, padded) * scale - old[:, lanes], 0.0)
    parts = []
    for k in range(count):
        source = system if k == 0 else work
        block = source[at(k), at(k)]

        def invert(bound, steps, **options):
            inv_h[at(k), :], inv_l[at(k), :] = split(inverse(block, eye, bound, steps, **options))

        if k == 0:
            invert(2.0 * step, 7)
        else:
            small = jnp.max(jnp.sum(jnp.abs(block - ridge * eye), axis=0)) <= 6.0
            pl.when(small)(functools.partial(invert, 6.0, 4, correct=False))
            pl.when(jnp.logical_not(small))(functools.partial(invert, 2.0 * step, 7, loop=True))
        x = inv_h[at(k), :], inv_l[at(k), :]
        column = product(split(source[(k + 1) * step :, at(k)]), x)
        parts.append(column[-padded:])
        if k == count - 1:
            break
        after = slice((k + 1) * step, width)
        column = split(column)
        low_h[after, at(k)], low_l[after, at(k)] = column[0][:-padded], column[1][:-padded]
        row = split(source[at(k), after])
        up_h[at(k), after], up_l[at(k), after] = row
        work[(k + 1) * step :, after] = source[(k + 1) * step :, after] - product(column, row)

    def backward(parts):
        for k in reversed(range(1, count)):
            before = slice(0, k * step)
            less = product(split(parts[k]), (low_h[at(k), before], low_l[at(k), before]))
            for i in range(k):
                parts[i] = parts[i] - less[:, i * step : (i + 1) * step]
        return parts

    def apply(parts):
        for k in range(count):
            now = parts[k] = product(split(parts[k]), (inv_h[at(k), :], inv_l[at(k), :]))
            if k < count - 1:
                after = slice((k + 1) * step, width)
                less = product(split(now), (up_h[at(k), after], up_l[at(k), after]))
                for i in range(k + 1, count):
                    parts[i] = parts[i] - less[:, (i - k - 1) * step : (i - k) * step]
        return backward(parts)

    for k, part in enumerate(backward(parts)):
        found[:, at(k)] = part

    def refine(state):
        short = system[width:, :] - wide_product(found[...], system)
        moved, size = 0.0, 0.0
        for k, part in enumerate(apply([short[:, at(k)] for k in range(count)])):
            found[:, at(k)] += part
            moved += jnp.sum(part * part)
            size += jnp.sum(found[:, at(k)] * found[:, at(k)])
        return state[0] + 1, jnp.logical_not((moved <= 1e-6 * size) & (size < 1e30))

    _, rough = lax.while_loop(lambda state: state[1] & (state[0] < 3), refine, (0, True))

    @pl.when(rough)
    def _():
        found[...] = jnp.zeros_like(found)
        gained, short, ahead = (slice(i * padded, (i + 1) * padded) for i in range(3))
        tiny = 1e-30

        def norms(there):
            return jnp.sum(work[there, :] * work[there, :], axis=1, keepdims=True)

        def restart(_, carry):
            work[short, :] = system[width:, :] - exact_product(found[...], system[:width, :])
            work[ahead, :] = work[short, :]
            work[gained, :] = jnp.zeros_like(found)
            first = norms(short)

            def advance(state):
                turn, _, size = state
                image = exact_product(work[ahead, :], system[:width, :])
                far = size / jnp.maximum(jnp.sum(work[ahead, :] * image, axis=1, keepdims=True), tiny)
                work[gained, :] += far * work[ahead, :]
                work[short, :] -= far * image
                after = norms(short)
                work[ahead, :] = work[short, :] + after / jnp.maximum(size, tiny) * work[ahead, :]
                return turn + 1, jnp.max(after - 1e-12 * first) > 0.0, after

            lax.while_loop(lambda state: state[1] & (state[0] < 500), advance, (0, True, first))
            found[...] += work[gained, :]
            return carry

        lax.fori_loop(0, 3, restart, 0)

    change = found[...]
    added = dot(change.astype(bf16), turned[...])
    updated[...] = predictions[...] + added[:classes]
    at_row = lax.broadcasted_iota(jnp.int32, (2 * tile, 2 * tile), 0)
    at_lane = lax.broadcasted_iota(jnp.int32, (2 * tile, 2 * tile), 1)
    goal = (at_row % tile) // own_width * (2 * own_width) + at_row // tile * own_width + at_row % own_width
    order = (goal == at_lane).astype(bf16)
    for u in range(width // (2 * tile)):
        one, two = slice(u * tile, (u + 1) * tile), slice(width // 2 + u * tile, width // 2 + (u + 1) * tile)
        part = jnp.concatenate([found[:, one] + old[:, one], found[:, two] + old[:, two]], axis=1)
        high, low, last = (dot(piece, order) for piece in three(part))
        moved = (high + low) + last
        coeffs[:, 2 * u * tile : 2 * (u + 1) * tile] = moved[:classes]


def solve(place, mine, other, mine_old, other_old, turned, predictions, total_rows):
    width, (classes, rows) = turned.shape[0], predictions.shape
    here = pl.BlockSpec(memory_space=pltpu.VMEM)
    padded = -(-classes // 16) * 16
    return pl.pallas_call(
        functools.partial(solve_kernel, float(total_rows)),
        out_shape=(
            jax.ShapeDtypeStruct((classes, width), f32),
            jax.ShapeDtypeStruct((classes, rows), f32),
        ),
        in_specs=[pl.BlockSpec(memory_space=pltpu.SMEM)] + [here] * 6,
        out_specs=(here, here),
        scratch_shapes=[
            pltpu.VMEM((width + padded, width), f32),
            pltpu.VMEM((width + padded, width), f32),
            pltpu.VMEM((width, step), bf16),
            pltpu.VMEM((width, step), bf16),
            pltpu.VMEM((width, width), bf16),
            pltpu.VMEM((width, width), bf16),
            pltpu.VMEM((width, width), bf16),
            pltpu.VMEM((width, width), bf16),
            pltpu.VMEM((padded, width), f32),
            pltpu.VMEM((padded, width), f32),
        ],
        compiler_params=pltpu.CompilerParams(vmem_limit_bytes=38 * 1024 * 1024),
        name="solve",
    )(place, mine, other, mine_old, other_old, turned, predictions)


def exchange(x, axes):
    return lax.all_to_all(x, axes, 0, 0, tiled=True)


def gather(x, axes):
    return exchange(jnp.broadcast_to(x[None], (lax.axis_size(axes), *x.shape)), axes)


def swap(x):
    return lax.ppermute(x, "core", [(0, 1), (1, 0)])


def local(frames, freqs, phase, labels, predictions, coeffs_old):
    rows, classes = predictions.shape
    depth, own = freqs.shape
    width = phase.shape[0]
    cores = lax.axis_size("core")
    devices = width // own
    place = lax.axis_index("core").astype(jnp.int32)[None]
    first = lax.reduce_precision(coeffs_old, 8, 7)
    second = lax.reduce_precision(coeffs_old - first, 8, 7)
    olds = [part.astype(bf16) for part in (first, second, coeffs_old - first - second)]
    filled = -(-(depth + 3 * (classes - tile)) // tile) * tile
    lanes = filled + 3 * tile

    def put(x, start):
        return jnp.pad(x, ((0, 0), (start, lanes - start - x.shape[1])))

    sent = put(freqs.T, 0)
    for i, part in enumerate(olds):
        sent += put(part[:, tile:], depth + i * (classes - tile)) + put(part[:, :tile], filled + i * tile)
    mine_sent = gather(sent, "z").reshape(-1, sent.shape[1])
    mine_sent = gather(mine_sent, ("x", "y")).reshape(width // cores, sent.shape[1])
    other_sent = swap(mine_sent)
    turned, keep, send = moments(
        place, mine_sent, other_sent, frames.T, phase[None, :], labels[None, :], predictions.T
    )
    shares = lax.axis_size("z")
    sums = (keep + swap(send)).reshape(lax.axis_size(("x", "y")), -1, tile)
    sums = exchange(sums, ("x", "y")).sum(0)
    share = sums.shape[0]
    sums = jnp.pad(sums, ((0, -share % (8 * shares)), (0, 0)))
    sums = exchange(sums.reshape(shares, -1, tile), "z").sum(0)
    sums = gather(sums, "z").reshape(-1, tile)[:share]
    mine = gather(sums, ("x", "y")).reshape(-1, tile)
    other = swap(mine)
    coeffs_new, new_predictions = solve(
        place, mine, other, mine_sent, other_sent, turned, predictions.T, rows * devices
    )
    return new_predictions.T, coeffs_new.T


def solution(mesh):
    chips = mesh.devices.reshape(4, 4, 8, 2)
    inner = Mesh(chips, ("x", "y", "z", "core"))
    every = ("x", "y", "z", "core")
    placed = (P(every, None), P(None, every), P(), P(every), P(every, None), P(every, None))
    return jax.shard_map(
        local, mesh=inner, in_specs=placed, out_specs=(P(every, None), P()), check_vma=False
    )
```
